32 devices in a mesh: dom: 16 (over z, y, core), rec: 2 (over x).
Axes of the slice: x: 2, y: 2, z: 4, core: 2. Of those that a mesh axis runs over, the one named last changes fastest.
Arguments:
- features: float32 [16384, 512], P(('dom', 'rec')), may hold values from -6 to 6
- positions: float32 [3, 16384], P(None, ('dom', 'rec')), may hold values from 0 to 2
- value_one: float32 [512, 512], replicated, may hold values from -0.25 to 0.25
- output_one: float32 [512, 512], replicated, may hold values from -0.25 to 0.25
- radial_one: float32 [8, 512], replicated, may hold values from -6 to 6
- value_two: float32 [512, 512], replicated, may hold values from -0.25 to 0.25
- output_two: float32 [512, 512], replicated, may hold values from -0.25 to 0.25
- radial_two: float32 [8, 512], replicated, may hold values from -6 to 6
- charge_weight: float32 [512, 2], replicated, may hold values from -0.25 to 0.25
- return_weight: float32 [2, 512], replicated, may hold values from -4 to 4
- green_kernel: float32 [192, 2, 2, 192, 192], P('rec', None, None, None, 'dom'), may hold values from -24 to 24
- exports: int32 [32, 2, 3], P(('dom', 'rec')), may hold values from 0 to 7, as said below
- export_counts: int32 [32, 2], P(('dom', 'rec')), may hold values from 1 to 3, as said below
- brick_anchor: int32 [3, 256], P(None, ('dom', 'rec')), may hold values from 0 to 188, as said below
Outputs:
- updated: float32 [16384, 512], P(('dom', 'rec'))
The draws below stay inside these ranges and needn't reach their ends.
Inputs may be any that keep to these rules, and one draw needn't show every extreme that they name: `exports`: each entry names one of the 8 blocks of its own domain, counted from 0; the 3 entries of one domain and side are distinct. `export_counts`: the live entries of a list are its first ones. `brick_anchor`: A block's brick of 4 x 8 x 8 cells lies inside the grid, and its first coordinates lie within the planes of the grid's first dimension that the dom index holding the block holds.
All inputs are finite; a program needn't handle non-finite values.
Results may differ from the reference program's by a relative error of at most 0.0003.
Values sent between devices are 32-bit elements; how exact they have to be, the bound alone decides.
No kernel may reach another device: no remote copies, remote signals or barrier semaphores. Data moves between devices by JAX's collectives and lax.ppermute only.
A program may use at most 128 MiB of HBM per device.

```python
import jax
import jax.numpy as jnp
from jax import lax

F = 512
NR = 8
BA = 64
NH = 3
BLK_DEV = 8
G = 192
BX = 4
BY = 8
BZ = 8
DOMAINS = 32
BLOCKS = 256
ATOMS = 16384
N_DOM = 16
N_REC = 2


def draw_exports(key, part):
    key = jax.random.fold_in(key, 11)
    scores = jax.random.randint(key, (DOMAINS * 2, BLK_DEV), 0, 1 << 20) * BLK_DEV + jnp.arange(BLK_DEV, dtype=jnp.int32)[None]
    ranking = jnp.argsort(scores, axis=1).astype(jnp.int32)[:, :NH]
    chosen = ranking.reshape(DOMAINS, 2, NH)
    marked = jax.random.randint(jax.random.fold_in(key, 1), (2,), 0, DOMAINS)
    chosen = chosen.at[marked[0], 0].set(jnp.arange(BLK_DEV - NH, BLK_DEV, dtype=jnp.int32))
    chosen = chosen.at[marked[1], 1].set(jnp.arange(NH, dtype=jnp.int32))
    return chosen


def draw_export_counts(key, part):
    key = jax.random.fold_in(key, 12)
    counts = jax.random.randint(key, (DOMAINS, 2), 1, NH + 1)
    marked = jax.random.randint(jax.random.fold_in(key, 1), (2,), 0, DOMAINS)
    counts = counts.at[marked[0], 0].set(NH)
    counts = counts.at[marked[1], 1].set(1)
    return counts


def draw_brick_anchor(key, part):
    key = jax.random.fold_in(key, 13)
    slab_depth = G // N_DOM
    holder = jnp.arange(BLOCKS, dtype=jnp.int32) // BLK_DEV // N_REC
    first = holder * slab_depth + jax.random.randint(jax.random.fold_in(key, 1), (BLOCKS,), 0, slab_depth - BX + 1)
    second = jax.random.randint(jax.random.fold_in(key, 2), (BLOCKS,), 0, G - BY + 1)
    third = jax.random.randint(jax.random.fold_in(key, 3), (BLOCKS,), 0, G - BZ + 1)
    first = first.at[0].set(0).at[BLOCKS - 1].set(G - BX)
    return jnp.stack([first, second, third]).astype(jnp.int32)


def block_scale(key, shape, pieces, smallest, high):
    gain, own = 1.0, jax.random.fold_in(key, 6)
    for dim, blocks in pieces:
        draws = jnp.exp(jax.random.uniform(jax.random.fold_in(own, dim), (blocks,), jnp.float32, smallest / len(pieces), high / len(pieces)))
        gain = gain * jnp.repeat(draws, shape[dim] // blocks).reshape([-1 if axis == dim else 1 for axis in range(len(shape))])
    return gain


def bell_draw(stream_key, shape, width, most, cuts=(), kind=jnp.bfloat16):
    drawn = jax.random.normal(stream_key, shape, jnp.float32) * width
    if len(cuts) > 0:
        drawn = block_scale(stream_key, shape, cuts, -0.22, 0.18) * drawn
    return jnp.clip(drawn, min=-most, max=most).astype(kind)


def setup_inputs(seed: int = 0) -> dict:
    seeds = jax.random.split(jax.random.key(seed), 15)
    return {
        "features": bell_draw(seeds[0], (ATOMS, F), 1.0, 6.0, ((0, 32),), jnp.float32),
        "positions": jnp.clip(2.0 * jax.random.uniform(seeds[1], (3, ATOMS), jnp.float32) ** block_scale(seeds[1], (3, ATOMS), ((1, 32),), -0.2, 0.2), 0.0, 2.0),
        "value_one": bell_draw(seeds[2], (F, F), F ** -0.5, 0.25, (), jnp.float32),
        "output_one": bell_draw(seeds[3], (F, F), F ** -0.5, 0.25, (), jnp.float32),
        "radial_one": bell_draw(seeds[4], (NR, F), 1.0, 6.0, (), jnp.float32),
        "value_two": bell_draw(seeds[5], (F, F), F ** -0.5, 0.25, (), jnp.float32),
        "output_two": bell_draw(seeds[6], (F, F), F ** -0.5, 0.25, (), jnp.float32),
        "radial_two": bell_draw(seeds[7], (NR, F), 1.0, 6.0, (), jnp.float32),
        "charge_weight": bell_draw(seeds[8], (F, 2), F ** -0.5, 0.25, (), jnp.float32),
        "return_weight": bell_draw(seeds[9], (2, F), 2 ** -0.5, 4.0, (), jnp.float32),
        "green_kernel": bell_draw(seeds[10], (G, 2, 2, G, G), 4.0, 24.0, ((0, 2), (4, 16)), jnp.float32),
        "exports": draw_exports(jax.random.fold_in(seeds[14], 71), 0),
        "export_counts": draw_export_counts(jax.random.fold_in(seeds[14], 71), 0),
        "brick_anchor": draw_brick_anchor(jax.random.fold_in(seeds[14], 71), 0),
    }


exact_mode = lax.Precision.HIGHEST
sharp_factor = 2.0
radial_reach = 3.0
soften = 0.01
norm_epsilon = 1e-05

def radial_basis(squared, levels):
    centers = jnp.arange(levels, dtype=jnp.float32) * (radial_reach / (levels - 1))
    distance = jnp.sqrt(squared + soften)
    shaped = centers.reshape((levels,) + (1,) * squared.ndim)
    return jnp.exp(-sharp_factor * (distance[None] - shaped) ** 2)

def block_messages(own_values, own_places, ghost_values, ghost_places, live_atoms, radial_weight):
    blocks = own_values.shape[0]
    members = own_values.shape[1]
    partner_values = jnp.concatenate([own_values, jnp.broadcast_to(ghost_values[None], (blocks,) + ghost_values.shape)], axis=1)
    partner_places = jnp.concatenate([own_places, jnp.broadcast_to(ghost_places[:, None], (3, blocks, ghost_places.shape[1]))], axis=2)
    squared = lax.optimization_barrier(jnp.sum((own_places[:, :, :, None] - partner_places[:, :, None, :]) ** 2, axis=0))
    kept_pairs = jnp.concatenate([1.0 - jnp.eye(members, dtype=jnp.float32), jnp.broadcast_to(live_atoms[None], (members, live_atoms.shape[0]))], axis=1)
    radial_terms = radial_basis(squared, radial_weight.shape[0]) * kept_pairs
    gathered = jnp.einsum('kbip,bpf->kbif', radial_terms, partner_values, precision=exact_mode)
    return jnp.einsum('kbif,kf->bif', gathered, radial_weight, precision=exact_mode)

def interaction(hidden, positions, value_weight, output_weight, radial_weight, exports, export_counts):
    values = jnp.dot(hidden, value_weight, precision=exact_mode, preferred_element_type=jnp.float32)
    value_blocks = values.reshape(BLOCKS, BA, F)
    place_blocks = positions.reshape(3, BLOCKS, BA)
    slot_index = jnp.arange(NH, dtype=jnp.int32)

    def one_domain(domain):
        below_domain = (domain + DOMAINS - 1) % DOMAINS
        above_domain = (domain + 1) % DOMAINS
        ghost_ids = jnp.concatenate([below_domain * BLK_DEV + exports[below_domain, 0], above_domain * BLK_DEV + exports[above_domain, 1]]).astype(jnp.int32)
        ghost_live = jnp.concatenate([slot_index < export_counts[below_domain, 0], slot_index < export_counts[above_domain, 1]]).astype(jnp.float32)
        ghost_values = value_blocks[ghost_ids].reshape(2 * NH * BA, F)
        ghost_places = place_blocks[:, ghost_ids].reshape(3, 2 * NH * BA)
        live_atoms = jnp.repeat(ghost_live, BA)
        own_blocks = (domain * BLK_DEV + jnp.arange(BLK_DEV, dtype=jnp.int32)).astype(jnp.int32)
        return block_messages(value_blocks[own_blocks], place_blocks[:, own_blocks], ghost_values, ghost_places, live_atoms, radial_weight)
    messages = lax.map(one_domain, jnp.arange(DOMAINS, dtype=jnp.int32)).reshape(ATOMS, F)
    scaled = messages * lax.rsqrt(lax.optimization_barrier(jnp.mean(messages * messages, axis=-1, keepdims=True)) + norm_epsilon)
    return hidden + jnp.dot(jax.nn.silu(scaled), output_weight, precision=exact_mode, preferred_element_type=jnp.float32)

def spline_window(coordinate, extent):
    cells = jnp.arange(extent, dtype=jnp.float32)[:, None]
    return jnp.exp(-(cells - coordinate[None] * ((extent - 1) / 2.0)) ** 2)

def atom_potentials(features, positions, charge_weight, green_kernel, brick_anchor):
    charges = jnp.einsum('af,fc->ca', features, charge_weight, precision=exact_mode)
    along_x = spline_window(positions[0], BX)
    along_y = spline_window(positions[1], BY)
    along_z = spline_window(positions[2], BZ)
    left_side = (charges[:, None] * along_x[None]).reshape(2 * BX, BLOCKS, BA)
    right_side = (along_y[:, None] * along_z[None]).reshape(BY * BZ, BLOCKS, BA)
    bricks = jnp.einsum('pba,qba->bpq', left_side, right_side, precision=exact_mode).reshape(BLOCKS, 2, BX, BY, BZ)
    anchor_zero = jnp.zeros((), jnp.int32)

    def corner_of(index):
        return (anchor_zero, brick_anchor[0, index].astype(jnp.int32), brick_anchor[1, index].astype(jnp.int32), brick_anchor[2, index].astype(jnp.int32))

    def deposit(index, grid):
        corner = corner_of(index)
        return lax.dynamic_update_slice(grid, lax.dynamic_slice(grid, corner, (2, BX, BY, BZ)) + bricks[index], corner)
    charge_grid = lax.fori_loop(0, BLOCKS, deposit, jnp.zeros((2, G, G, G), jnp.float32))
    spectrum = jnp.fft.fftn(charge_grid, axes=(1, 2, 3))
    mixed_real = jnp.einsum('zcdxy,dxyz->cxyz', green_kernel, jnp.real(spectrum), precision=exact_mode)
    mixed_imag = jnp.einsum('zcdxy,dxyz->cxyz', green_kernel, jnp.imag(spectrum), precision=exact_mode)
    potential_grid = jnp.real(jnp.fft.ifftn(lax.complex(mixed_real, mixed_imag), axes=(1, 2, 3)))

    def brick_at(index):
        return lax.dynamic_slice(potential_grid, corner_of(index), (2, BX, BY, BZ))
    picked = lax.map(brick_at, jnp.arange(BLOCKS, dtype=jnp.int32)).reshape(BLOCKS, 2, BX, BY * BZ)
    partial_sums = jnp.einsum('bcxq,qba->bcxa', picked, right_side, precision=exact_mode)
    return jnp.einsum('bcxa,xba->cba', partial_sums, along_x.reshape(BX, BLOCKS, BA), precision=exact_mode).reshape(2, ATOMS)

def reference(features, positions, value_one, output_one, radial_one, value_two, output_two, radial_two, charge_weight, return_weight, green_kernel, exports, export_counts, brick_anchor):
    hidden_one = interaction(features, positions, value_one, output_one, radial_one, exports, export_counts)
    atom_potential = atom_potentials(features, positions, charge_weight, green_kernel, brick_anchor)
    layer_input = hidden_one + jnp.einsum('ca,cf->af', atom_potential, return_weight, precision=exact_mode)
    return interaction(layer_input, positions, value_two, output_two, radial_two, exports, export_counts)
```

```python
import functools
import math

import jax
import jax.numpy as jnp
import numpy as np
from jax import lax
from jax.experimental import pallas as pl
from jax.experimental.pallas import tpu as pltpu
from jax.sharding import PartitionSpec as P

BA = 64
BX = 4
BY = 8
BZ = 8
NB = 8
NH = 3
NR = 8
LANES = 128

soften = 0.01
norm_epsilon = 1e-05
f32 = jnp.float32
bf16 = jnp.bfloat16
NN = (((1,), (0,)), ((), ()))
NT = (((1,), (1,)), ((), ()))
STEP = 12.0 / 7.0
FACTORS = np.exp(-18.0 * np.arange(NR) ** 2 / 49.0).astype(np.float32)


def params(mib=60):
    return pltpu.CompilerParams(vmem_limit_bytes=mib * 1024 * 1024)


def split(value):
    high = value.astype(bf16)
    return high, (value - high.astype(f32)).astype(bf16)


def product(left, right, dims=NN):
    def one(a, b):
        return lax.dot_general(a, b, dims, preferred_element_type=f32)

    return one(left[0], right[0]) + (one(left[0], right[1]) + one(left[1], right[0]))


def wave(phase, period):
    rest = phase - period * jnp.floor(phase * (1.0 / period) + 0.5)
    turn = rest * (1.0 / period)
    square = turn * turn
    cosine = jnp.full_like(turn, (-1) ** 9 * (2 * math.pi) ** 18 / math.factorial(18))
    sine = jnp.full_like(turn, (-1) ** 9 * (2 * math.pi) ** 19 / math.factorial(19))
    for n in range(8, -1, -1):
        cosine = cosine * square + (-1) ** n * (2 * math.pi) ** (2 * n) / math.factorial(2 * n)
        sine = sine * square + (-1) ** n * (2 * math.pi) ** (2 * n + 1) / math.factorial(2 * n + 1)
    return cosine, sine * turn


def rows_iota(shape):
    return lax.broadcasted_iota(jnp.int32, shape, len(shape) - 2)


def lanes_iota(shape):
    return lax.broadcasted_iota(jnp.int32, shape, len(shape) - 1)


def pack_places(out_ref, places_ref, exports_ref, counts_ref, side):
    base = NH * BA
    out_ref[base : base + 8, :] = jnp.zeros((8, out_ref.shape[1]), f32)
    for s in range(NH):
        chosen = exports_ref[0, side, s]
        lane = side * base + s * BA
        found = places_ref[:, :BA]
        for b in range(1, NB):
            found = jnp.where(chosen == b, places_ref[:, b * BA : (b + 1) * BA], found)
        out_ref[base : base + 3, lane : lane + BA] = found
        live = jnp.where(s < counts_ref[0, side], 1.0, 0.0)
        out_ref[base + 3 : base + 4, lane : lane + BA] = jnp.full((1, BA), live, f32)


def pack_rows(out_ref, rows_ref, exports_ref, side):
    for s in range(NH):
        start = pl.multiple_of(exports_ref[0, side, s] * BA, BA)
        out_ref[s * BA : (s + 1) * BA, :] = rows_ref[pl.ds(start, BA), :]


def head_kernel(
    features_ref, places_ref, charge_ref, anchor_ref, exports_ref, counts_ref,
    up_ref, down_ref, payload_ref,
    staged,
):
    for out_ref, side in ((up_ref, 0), (down_ref, 1)):
        pack_rows(out_ref, features_ref, exports_ref, side)
        pack_places(out_ref, places_ref, exports_ref, counts_ref, side)
    width = charge_ref.shape[0]
    charge_rows = jnp.transpose(
        jnp.concatenate([charge_ref[...], jnp.zeros((width, 6), f32)], axis=1)
    )
    charges = product(split(charge_rows), split(features_ref[...]), NT)
    chunks = features_ref.shape[0] // LANES
    for t in range(chunks):
        lane = slice(t * LANES, (t + 1) * LANES)
        for c in range(2):
            staged[c * chunks + t : c * chunks + t + 1, :] = charges[c : c + 1, lane]
        for d in range(3):
            row = (2 + d) * chunks + t
            staged[row : row + 1, :] = places_ref[d : d + 1, lane]
    anchors = anchor_ref[...].astype(f32)
    block = lanes_iota((3, LANES)) % (NB * BZ) // BZ
    spread = jnp.broadcast_to(anchors[:, :1], (3, LANES))
    for b in range(1, NB):
        spread = jnp.where(block == b, anchors[:, b : b + 1], spread)
    staged[5 * chunks : 5 * chunks + 3, :] = spread
    lane = lanes_iota((1, LANES))
    listed = jnp.zeros((1, LANES), jnp.int32)
    for side in range(2):
        for s in range(NH):
            listed = jnp.where(lane == side * NH + s, exports_ref[0, side, s], listed)
    staged[5 * chunks + 3 :, :] = listed.astype(f32)
    payload = staged[...]

    @pl.loop(0, payload_ref.shape[0])
    def _(domain):
        payload_ref[domain] = payload


def pair_terms(squared, live):
    softened = squared + soften
    near = jnp.exp(-2.0 * softened)
    if live is not None:
        near = near * live
    return near, jnp.exp(STEP * jnp.sqrt(softened))


def squared_distance(columns, rows):
    total = None
    for d in range(3):
        delta = columns[:, d : d + 1] - rows[d : d + 1, :]
        total = delta * delta if total is None else total + delta * delta
    return total


def all_messages(values_ref, ghost_values_ref, places_ref, ghost_places, weight_ref, out_ref):
    weights = [weight_ref[k : k + 1, :] * float(FACTORS[k]) for k in range(NR)]
    atoms = values_ref.shape[0]
    columns = jnp.transpose(
        jnp.concatenate([places_ref[...], jnp.zeros((5, atoms), f32)], axis=0)
    )
    ghosts = 2 * NH * BA
    near, ratio = pair_terms(
        squared_distance(columns, ghost_places[:, :ghosts]), ghost_places[3:4, :ghosts]
    )
    ghost_values = ghost_values_ref[...]
    total = None
    term = near
    for k in range(0, NR, 2):
        after = term * ratio
        left = split(jnp.concatenate([term, after], axis=1))
        right = split(
            jnp.concatenate(
                [ghost_values * weights[k], ghost_values * weights[k + 1]],
                axis=0,
            )
        )
        part = product(left, right)
        total = part if total is None else total + part
        term = after * ratio
    out_ref[...] = total
    half = lanes_iota((BA, 2 * BA)) >= BA
    partner = lanes_iota((BA, 2 * BA)) % BA
    other = (partner != rows_iota((BA, 2 * BA))).astype(f32)
    for b in range(atoms // BA):
        rows = slice(b * BA, (b + 1) * BA)
        here = places_ref[:, rows]
        near, ratio = pair_terms(
            squared_distance(columns[rows], jnp.concatenate([here, here], axis=1)), other
        )
        term = jnp.where(half, near * ratio, near)
        ratio = ratio * ratio
        lefts, rights = [], []
        values = values_ref[rows, :]
        for k in range(0, NR, 2):
            lefts.append(term)
            rights.append(values * weights[k])
            rights.append(values * weights[k + 1])
            term = term * ratio
        out_ref[rows, :] += product(
            split(jnp.concatenate(lefts, axis=1)), split(jnp.concatenate(rights, axis=0))
        )


def finish(hidden, messages, output_ref):
    scaled = messages * lax.rsqrt(
        jnp.mean(messages * messages, axis=-1, keepdims=True) + norm_epsilon
    )
    active = scaled / (1.0 + jnp.exp(-scaled))
    return hidden + product(split(active), split(output_ref[...]))


def first_layer_kernel(
    features_ref, up_ref, down_ref, places_ref, value_one_ref, output_one_ref, weight_ref,
    value_two_ref, exports_ref,
    hidden_ref, values_two_ref, up_two_ref, down_two_ref, ghost_places_ref,
    values, ghost_values, messages,
):
    base = NH * BA
    value_weight = split(value_one_ref[...])
    values[...] = product(split(features_ref[...]), value_weight)
    ghost_values[:base, :] = product(split(up_ref[:base, :]), value_weight)
    ghost_values[base:, :] = product(split(down_ref[:base, :]), value_weight)
    ghost_places_ref[...] = up_ref[base : base + 8, :] + down_ref[base : base + 8, :]
    ghost_places = ghost_places_ref[...]
    all_messages(values, ghost_values, places_ref, ghost_places, weight_ref, messages)
    hidden_ref[...] = finish(features_ref[...], messages[...], output_one_ref)
    values_two_ref[...] = product(split(hidden_ref[...]), split(value_two_ref[...]))
    pack_rows(up_two_ref, values_two_ref, exports_ref, 0)
    pack_rows(down_two_ref, values_two_ref, exports_ref, 1)


def second_layer_kernel(
    values_ref, up_two_ref, down_two_ref, ghost_places_ref, places_ref, weight_ref,
    return_ref, value_two_ref,
    messages_ref, returned_ref,
    ghost_values,
):
    base = NH * BA
    ghost_values[:base, :] = up_two_ref[...]
    ghost_values[base:, :] = down_two_ref[...]
    ghost_places = ghost_places_ref[...]
    all_messages(values_ref, ghost_values, places_ref, ghost_places, weight_ref, messages_ref)
    return_rows = jnp.concatenate(
        [return_ref[...], jnp.zeros((6, return_ref.shape[1]), f32)], axis=0
    )
    returned_ref[...] = product(split(return_rows), split(value_two_ref[...]))


def tail_kernel(
    received_ref, messages_ref, hidden_ref, ghost_places_ref, places_ref, weight_ref,
    return_ref, returned_ref, output_two_ref,
    updated_ref,
):
    atoms = hidden_ref.shape[0]
    ghosts = 2 * NH * BA
    potentials = jnp.sum(received_ref[...], axis=0)
    columns = jnp.transpose(potentials)
    ghost_places = ghost_places_ref[...]
    ghost_columns = jnp.transpose(ghost_places[:, :ghosts])
    own_columns = jnp.transpose(
        jnp.concatenate([places_ref[...], jnp.zeros((5, atoms), f32)], axis=0)
    )
    half = lanes_iota((BA, LANES)) >= BA
    other = (lanes_iota((BA, LANES)) % BA != rows_iota((BA, LANES))).astype(f32)
    ghost_potential = [
        jnp.concatenate([columns[c * BA : (c + 1) * BA, NB + s : NB + s + 1] for s in range(2 * NH)], axis=0)
        for c in range(2)
    ]
    pieces = []
    for t in range(atoms // LANES):
        lane = slice(t * LANES, (t + 1) * LANES)
        here = places_ref[:, lane]
        near, ratio = pair_terms(squared_distance(ghost_columns, here), ghost_columns[:, 3:4])
        squared = None
        own_potential = []
        for c in range(2):
            own_potential.append(
                jnp.where(
                    half,
                    columns[c * BA : (c + 1) * BA, 2 * t + 1 : 2 * t + 2],
                    columns[c * BA : (c + 1) * BA, 2 * t : 2 * t + 1],
                )
            )
        for d in range(3):
            first = own_columns[2 * t * BA : (2 * t + 1) * BA, d : d + 1]
            second = own_columns[(2 * t + 1) * BA : (2 * t + 2) * BA, d : d + 1]
            delta = jnp.where(half, second, first) - here[d : d + 1, :]
            squared = delta * delta if squared is None else squared + delta * delta
        own_near, own_ratio = pair_terms(squared, other)
        ratio = jnp.concatenate([ratio, own_ratio], axis=0)
        terms = [
            jnp.concatenate([near * ghost_potential[c], own_near * own_potential[c]], axis=0)
            for c in range(2)
        ]
        sums = []
        for k in range(NR):
            for c in range(2):
                sums.append(jnp.sum(terms[c], axis=0, keepdims=True))
                if k + 1 < NR:
                    terms[c] = terms[c] * ratio
        pieces.append(jnp.concatenate(sums, axis=0))
    gathered = jnp.transpose(jnp.concatenate(pieces, axis=1))
    spread = jnp.concatenate(
        [
            returned_ref[c : c + 1, :] * (weight_ref[k : k + 1, :] * float(FACTORS[k]))
            for k in range(NR)
            for c in range(2)
        ],
        axis=0,
    )
    messages = messages_ref[...] + product(split(gathered), split(spread))
    back = [return_ref[c : c + 1, :] for c in range(2)]
    layer_input = jnp.concatenate(
        [
            hidden_ref[b * BA : (b + 1) * BA, :]
            + columns[:BA, b : b + 1] * back[0]
            + columns[BA:, b : b + 1] * back[1]
            for b in range(atoms // BA)
        ],
        axis=0,
    )
    updated_ref[...] = finish(layer_input, messages, output_two_ref)


def transform_tables(grid):
    half = grid // 2
    u = np.arange(grid)
    x = np.concatenate([np.arange(half + 1), np.arange(1, half)])
    angle = 2.0 * np.pi * (np.outer(u, x) % grid) / grid
    table = np.where(np.arange(grid)[None] <= half, np.cos(angle), np.sin(angle)).astype(np.float32)
    back = (table.T / float(grid) ** 3).astype(np.float32)
    return table, back


def reciprocal_kernel(
    grid, slabs, per_slab, second, depth,
    place_ref, exports_ref, payload_ref, green_ref, forward_ref, back_ref,
    out_ref,
    planes, turns_high, turns_low, spread_high, spread_low, brick, carry,
    shift_cos, shift_sin, stage_cos, stage_sin, chosen, potential,
):
    domains = slabs * per_slab
    half = grid // 2
    thick = grid // slabs
    starts = thick - BX + 1
    rows = 2 * second
    cells = per_slab * NB * BZ
    atoms = per_slab * NB * BA
    chunks = atoms // LANES
    own = NB * BA // LANES
    wide = depth
    first_v = (place_ref[0] * second).astype(f32)
    first_w = (place_ref[1] * place_ref[2]).astype(f32)
    period = float(grid)

    row = rows_iota((rows, 1))
    frequency = jnp.where(row >= second, row - second, row).astype(f32) + first_v
    cosine, sine = wave(jnp.broadcast_to(frequency, (rows, LANES)), period)
    shift_cos[...] = cosine
    shift_sin[...] = sine
    upper = rows_iota((rows, LANES)) >= second
    spread_high[...] = jnp.zeros(spread_high.shape, bf16)
    spread_low[...] = jnp.zeros(spread_low.shape, bf16)
    carry[...] = jnp.zeros(carry.shape, f32)
    left_half = lanes_iota((1, LANES)) < LANES // 2

    def atom_rows(slab, t):
        base = slab * per_slab + t // own
        return [payload_ref[base, q * own + t % own : q * own + t % own + 1, :] for q in range(5)]

    def windows(parts):
        cell = rows_iota((BY, LANES)).astype(f32)
        along_x = [jnp.exp(-((float(i) - parts[2] * 1.5) ** 2)) for i in range(BX)]
        along_y = jnp.exp(-((cell - parts[3] * 3.5) ** 2))
        along_z = jnp.exp(-((cell - parts[4] * 3.5) ** 2))
        return along_x, along_y, along_z

    def anchor(slab, dim):
        found = []
        for q in range(0, per_slab, 2):
            one = payload_ref[slab * per_slab + q, 5 * own + dim : 5 * own + dim + 1, :]
            two = payload_ref[slab * per_slab + q + 1, 5 * own + dim : 5 * own + dim + 1, :]
            found.append(jnp.where(left_half, one, two))
        return jnp.concatenate(found, axis=1) if len(found) > 1 else found[0]

    def fill_spread(slab):
        both = []
        for t in range(chunks):
            parts = atom_rows(slab, t)
            along = windows(parts)
            along_z = along[2]
            masked = jnp.concatenate(
                [jnp.where(left_half, along_z, 0.0), jnp.where(left_half, 0.0, along_z)], axis=0
            )
            high, low = split(masked)
            spread_high[t * 16 : (t + 1) * 16, t * LANES : (t + 1) * LANES] = high
            spread_low[t * 16 : (t + 1) * 16, t * LANES : (t + 1) * LANES] = low
            both.append((parts, along))
        return both

    def slab_masks(slab):
        start = anchor(slab, 0) - (slab * thick).astype(f32)
        return [(start == float(s)).astype(f32) for s in range(starts)]

    def deposit(slab):
        both = fill_spread(slab)
        lefts = []
        for parts, (along_x, along_y, _) in both:
            lefts.append(
                jnp.concatenate(
                    [(parts[c] * along_x[i]) * along_y for c in range(2) for i in range(BX)], axis=0
                )
            )
        brick[...] = product(
            split(jnp.concatenate(lefts, axis=1)), (spread_high[...], spread_low[...]), NT
        )
        low_cell = anchor(slab, 2) + (lanes_iota((1, cells)) % BZ).astype(f32)
        ramp = rows_iota((8, cells)).astype(f32) + first_w
        cosine, sine = wave(ramp * low_cell, period)
        turn_cos, turn_sin = wave(8.0 * low_cell, period)
        for g in range(wide // 8):
            at = slice(g * 8, (g + 1) * 8)
            stage_cos[at, :] = cosine
            stage_sin[at, :] = sine
            cosine, sine = cosine * turn_cos - sine * turn_sin, cosine * turn_sin + sine * turn_cos
        cos_high, cos_low = split(stage_cos[...])
        sin_high, sin_low = split(stage_sin[...])
        for ref, c_part, s_part in ((turns_high, cos_high, sin_high), (turns_low, cos_low, sin_low)):
            ref[slab, :wide, :cells] = c_part
            ref[slab, :wide, cells:] = s_part
            ref[slab, wide:, :cells] = -s_part
            ref[slab, wide:, cells:] = c_part
        wide_cos = jnp.concatenate([shift_cos[...]] * (cells // LANES), axis=1)
        wide_sin = jnp.concatenate([shift_sin[...]] * (cells // LANES), axis=1)
        top = jnp.concatenate([upper] * (cells // LANES), axis=1) if cells > LANES else upper
        cosine, sine = wave(frequency * anchor(slab, 1), period)
        real = [jnp.zeros((rows, cells), f32)] * BX
        imag = [jnp.zeros((rows, cells), f32)] * BX
        for j in range(BY):
            for i in range(BX):
                low = brick[i * BY + j : i * BY + j + 1, :]
                high = brick[(BX + i) * BY + j : (BX + i) * BY + j + 1, :]
                weight = jnp.where(top, high, low)
                real[i] = real[i] + weight * cosine
                imag[i] = imag[i] - weight * sine
            if j + 1 < BY:
                cosine, sine = (
                    cosine * wide_cos - sine * wide_sin,
                    cosine * wide_sin + sine * wide_cos,
                )
        masks = slab_masks(slab)
        placed = []
        for x in range(thick):
            parts = []
            for source in (real, imag):
                total = None
                for i in range(BX):
                    if 0 <= x - i < starts:
                        piece = source[i] * masks[x - i]
                        total = piece if total is None else total + piece
                parts.append(total)
            placed.append(jnp.concatenate(parts, axis=1))
        return product(
            split(jnp.concatenate(placed, axis=0)), (turns_high[slab], turns_low[slab]), NT
        )

    def put(x, value):
        planes[:, pl.ds(x, 1), :] = value[:, None, :]

    def get(x):
        return planes[:, pl.ds(x, 1), :][:, 0, :]

    def swapped(value):
        return jnp.concatenate([value[:, wide:], -value[:, :wide]], axis=1)

    @pl.loop(0, slabs // 2)
    def _(m):
        near = deposit(m)
        far = deposit(slabs - 1 - m)
        for r in range(thick):
            x = m * thick + r
            one = near[r * rows : (r + 1) * rows]
            if r == 0:
                two = carry[...]
            else:
                two = far[(thick - r) * rows : (thick - r + 1) * rows]
            put(x, one + two)
            put(half + x, swapped(one - two))
        carry[...] = far[:rows]

    put(half, carry[...])

    def padded(kernel):
        gap = wide - kernel.shape[1]
        if gap == 0:
            return kernel
        return jnp.concatenate([kernel, jnp.zeros((kernel.shape[0], gap), f32)], axis=1)

    table = split(forward_ref[...])
    table_back = split(back_ref[...])

    @pl.loop(0, second)
    def _(v):
        inside = jnp.concatenate([planes[v], planes[second + v]], axis=1)
        spectrum = product(table, split(inside))
        outside = []
        for c in range(2):
            zero, one = padded(green_ref[v, c, 0]), padded(green_ref[v, c, 1])
            for part in range(2):
                outside.append(
                    zero * spectrum[:, part * wide : (part + 1) * wide]
                    + one * spectrum[:, (2 + part) * wide : (3 + part) * wide]
                )
        result = product(table_back, split(jnp.concatenate(outside, axis=1)))
        planes[v] = result[:, : 2 * wide]
        planes[second + v] = result[:, 2 * wide :]

    def evaluate(slab, inputs):
        masks = slab_masks(slab)
        both = fill_spread(slab)
        found = product(
            split(jnp.concatenate(inputs, axis=0)), (turns_high[slab], turns_low[slab])
        )
        twice = [jnp.concatenate([mask, mask], axis=1) for mask in masks]
        for i in range(BX):
            total = None
            for s in range(starts):
                piece = found[(s + i) * rows : (s + i + 1) * rows] * twice[s]
                total = piece if total is None else total + piece
            chosen[i * rows : (i + 1) * rows, :] = total
        cell = anchor(slab, 1) + rows_iota((BY, cells)).astype(f32)
        cosine, sine = wave(cell * first_v, period)
        turn_cos, turn_sin = wave(cell, period)
        sums = [jnp.zeros((BY, cells), f32)] * (2 * BX)
        for v in range(second):
            for c in range(2):
                for i in range(BX):
                    at = i * rows + c * second + v
                    sums[c * BX + i] = (
                        sums[c * BX + i]
                        + chosen[at : at + 1, :cells] * cosine
                        - chosen[at : at + 1, cells:] * sine
                    )
            if v + 1 < second:
                cosine, sine = cosine * turn_cos - sine * turn_sin, cosine * turn_sin + sine * turn_cos
        at_atoms = product(
            split(jnp.concatenate(sums, axis=0)), (spread_high[...], spread_low[...])
        )
        for t in range(chunks):
            lane = slice(t * LANES, (t + 1) * LANES)
            _, (along_x, along_y, _) = both[t]
            pair = []
            for c in range(2):
                total = None
                for i in range(BX):
                    at = (c * BX + i) * BY
                    piece = at_atoms[at : at + BY, lane] * along_x[i]
                    total = piece if total is None else total + piece
                pair.append(jnp.sum(total * along_y, axis=0, keepdims=True))
            one = jnp.where(left_half, pair[0], pltpu.roll(pair[1], LANES // 2, 1))
            two = jnp.where(left_half, pltpu.roll(pair[0], LANES // 2, 1), pair[1])
            potential[pl.ds(slab * per_slab * NB + 2 * t, 1), :] = one
            potential[pl.ds(slab * per_slab * NB + 2 * t + 1, 1), :] = two

    def straight(x):
        even = get(x)
        odd = get(jnp.minimum(half + x, grid - 1)) * jnp.where((x > 0) & (x < half), 1.0, 0.0)
        turned = jnp.concatenate([-odd[:, wide:], odd[:, :wide]], axis=1)
        return even + turned, even - turned

    @pl.loop(0, slabs // 2)
    def _(m):
        near, far = [], [None] * thick
        for r in range(thick):
            ahead, behind = straight(m * thick + r)
            near.append(ahead)
            if r > 0:
                far[thick - r] = behind
        far[0] = straight(m * thick + thick)[1]
        evaluate(m, near)
        evaluate(slabs - 1 - m, far)

    @pl.loop(0, domains)
    def _(domain):
        out_ref[domain, NB + 2 * NH :, :] = jnp.zeros((16 - NB - 2 * NH, LANES), f32)
        out_ref[domain, :NB, :] = potential[pl.ds(pl.multiple_of(domain * NB, NB), NB), :]
        below = lax.rem(domain + domains - 1, domains)
        above = lax.rem(domain + 1, domains)
        for s in range(NH):
            at = below * NB + exports_ref[below, s]
            out_ref[domain, NB + s : NB + s + 1, :] = potential[pl.ds(at, 1), :]
            at = above * NB + exports_ref[above, NH + s]
            out_ref[domain, NB + NH + s : NB + NH + s + 1, :] = potential[pl.ds(at, 1), :]


def build_reciprocal(grid, slabs, per_slab, second, depth):
    domains = slabs * per_slab
    cells = per_slab * NB * BZ
    slab_atoms = per_slab * NB * BA
    return pl.pallas_call(
        functools.partial(reciprocal_kernel, grid, slabs, per_slab, second, depth),
        in_specs=[SMEM, SMEM] + [VMEM] * 4,
        out_specs=VMEM,
        out_shape=jax.ShapeDtypeStruct((domains, 16, LANES), f32),
        scratch_shapes=[
            pltpu.VMEM((2 * second, grid, 2 * depth), f32),
            pltpu.VMEM((slabs, 2 * depth, 2 * cells), bf16),
            pltpu.VMEM((slabs, 2 * depth, 2 * cells), bf16),
            pltpu.VMEM((cells, slab_atoms), bf16),
            pltpu.VMEM((cells, slab_atoms), bf16),
            pltpu.VMEM((2 * BX * BY, cells), f32),
            pltpu.VMEM((2 * second, 2 * depth), f32),
            pltpu.VMEM((2 * second, LANES), f32),
            pltpu.VMEM((2 * second, LANES), f32),
            pltpu.VMEM((depth, cells), f32),
            pltpu.VMEM((depth, cells), f32),
            pltpu.VMEM((BX * 2 * second, 2 * cells), f32),
            pltpu.VMEM((domains * NB, LANES), f32),
        ],
        compiler_params=params(),
    )


VMEM = pl.BlockSpec(memory_space=pltpu.VMEM)
SMEM = pl.BlockSpec(memory_space=pltpu.SMEM)


def per_device(
    features,
    positions,
    value_one,
    output_one,
    radial_one,
    value_two,
    output_two,
    radial_two,
    charge_weight,
    return_weight,
    green_kernel,
    exports,
    export_counts,
    brick_anchor,
):
    axes = ("dom", "rec")
    slabs, per_slab = lax.axis_size("dom"), lax.axis_size("rec")
    domains = slabs * per_slab
    atoms, width = features.shape
    depth_rows, grid, second = green_kernel.shape[0], green_kernel.shape[3], green_kernel.shape[4]
    depth = -(-depth_rows // LANES) * LANES
    chunks = atoms // LANES
    payload_rows = 5 * chunks + 4
    base = NH * BA

    def shape(*dims):
        return jax.ShapeDtypeStruct(dims, f32)

    def around(rows, by):
        return lax.ppermute(rows, axes, [(i, (i + by) % domains) for i in range(domains)])

    up, down, payload = pl.pallas_call(
        head_kernel,
        in_specs=[VMEM] * 4 + [SMEM] * 2,
        out_specs=[VMEM] * 3,
        out_shape=[
            shape(base + 8, width), shape(base + 8, width), shape(domains, payload_rows, LANES)
        ],
        scratch_shapes=[pltpu.VMEM((payload_rows, LANES), f32)],
        compiler_params=params(),
    )(features, positions, charge_weight, brick_anchor, exports, export_counts)

    up, down, green_kernel = lax.optimization_barrier((up, down, green_kernel))
    green = jnp.transpose(green_kernel, (4, 1, 2, 3, 0))
    up = around(up, 1)
    down = around(down, -1)
    payload, green, up, down = lax.optimization_barrier((payload, green, up, down))
    everyone = lax.all_to_all(payload, axes, 0, 0, tiled=True)

    hidden, values_two, up_two, down_two, ghost_places = pl.pallas_call(
        first_layer_kernel,
        in_specs=[VMEM] * 8 + [SMEM],
        out_specs=[VMEM] * 5,
        out_shape=[
            shape(atoms, width), shape(atoms, width), shape(base, width), shape(base, width),
            shape(8, width),
        ],
        scratch_shapes=[
            pltpu.VMEM((atoms, width), f32),
            pltpu.VMEM((2 * base, width), f32),
            pltpu.VMEM((atoms, width), f32),
        ],
        compiler_params=params(),
    )(features, up, down, positions, value_one, output_one, radial_one, value_two, exports)

    everyone, hidden = lax.optimization_barrier((everyone, hidden))
    up_two = around(up_two, 1)
    down_two = around(down_two, -1)

    place = jnp.stack(
        [lax.axis_index("dom"), lax.axis_index("rec"), jnp.int32(depth_rows)]
    ).astype(jnp.int32)
    all_exports = everyone[:, 5 * chunks + 3, :8].astype(jnp.int32)
    table, table_back = transform_tables(grid)
    outgoing = build_reciprocal(grid, slabs, per_slab, second, depth)(
        place, all_exports, everyone, green, table, table_back
    )

    outgoing, up_two, down_two = lax.optimization_barrier((outgoing, up_two, down_two))
    received = lax.all_to_all(outgoing, axes, 0, 0, tiled=True)

    messages, returned = pl.pallas_call(
        second_layer_kernel,
        in_specs=[VMEM] * 8,
        out_specs=[VMEM] * 2,
        out_shape=[shape(atoms, width), shape(8, width)],
        scratch_shapes=[pltpu.VMEM((2 * base, width), f32)],
        compiler_params=params(),
    )(values_two, up_two, down_two, ghost_places, positions, radial_two, return_weight, value_two)

    return pl.pallas_call(
        tail_kernel,
        in_specs=[VMEM] * 9,
        out_specs=VMEM,
        out_shape=shape(atoms, width),
        compiler_params=params(),
    )(
        received, messages, hidden, ghost_places, positions, radial_two, return_weight, returned, output_two
    )


def solution(mesh):
    placed = (
        P(("dom", "rec"), None),
        P(None, ("dom", "rec")),
        P(),
        P(),
        P(),
        P(),
        P(),
        P(),
        P(),
        P(),
        P("rec", None, None, None, "dom"),
        P(("dom", "rec"), None, None),
        P(("dom", "rec"), None),
        P(None, ("dom", "rec")),
    )
    return jax.shard_map(
        per_device, mesh=mesh, in_specs=placed, out_specs=P(("dom", "rec"), None), check_vma=False
    )
```

```python
import functools
import math

import jax
import jax.numpy as jnp
import numpy as np
from jax import lax
from jax.experimental import pallas as pl
from jax.experimental.pallas import tpu as pltpu
from jax.sharding import PartitionSpec as P

BA = 64
BX = 4
BY = 8
BZ = 8
NB = 8
NH = 3
NR = 8
LANES = 128

soften = 0.01
norm_epsilon = 1e-05
f32 = jnp.float32
bf16 = jnp.bfloat16
NN = (((1,), (0,)), ((), ()))
NT = (((1,), (1,)), ((), ()))
STEP = 12.0 / 7.0
OWN_GROUP = 4
FACTORS = np.exp(-18.0 * np.arange(NR) ** 2 / 49.0).astype(np.float32)


def params(mib=60):
    return pltpu.CompilerParams(vmem_limit_bytes=mib * 1024 * 1024)


def split(value):
    high = value.astype(bf16)
    return high, (value - high.astype(f32)).astype(bf16)


def product(left, right, dims=NN):
    axis = dims[0][1][0]
    return lax.dot_general(
        jnp.concatenate([left[0], left[0], left[1]], axis=1),
        jnp.concatenate([right[0], right[1], right[0]], axis=axis),
        dims,
        preferred_element_type=f32,
    )


def narrow_product(left, right):
    def one(a, b):
        return lax.dot_general(a, b, NN, preferred_element_type=f32)

    return one(left[0], right[0]) + (one(left[0], right[1]) + one(left[1], right[0]))


def wave(phase, period):
    rest = phase - period * jnp.floor(phase * (1.0 / period) + 0.5)
    turn = rest * (1.0 / period)
    square = turn * turn
    cosine = jnp.full_like(turn, (-1) ** 9 * (2 * math.pi) ** 18 / math.factorial(18))
    sine = jnp.full_like(turn, (-1) ** 9 * (2 * math.pi) ** 19 / math.factorial(19))
    for n in range(8, -1, -1):
        cosine = cosine * square + (-1) ** n * (2 * math.pi) ** (2 * n) / math.factorial(2 * n)
        sine = sine * square + (-1) ** n * (2 * math.pi) ** (2 * n + 1) / math.factorial(2 * n + 1)
    return cosine, sine * turn


def rows_iota(shape):
    return lax.broadcasted_iota(jnp.int32, shape, len(shape) - 2)


def lanes_iota(shape):
    return lax.broadcasted_iota(jnp.int32, shape, len(shape) - 1)


def side_by_side(works):
    results = [None] * len(works)
    waiting = list(range(len(works)))
    while waiting:
        for n in list(waiting):
            try:
                next(works[n])
            except StopIteration as end:
                results[n] = end.value
                waiting.remove(n)
    return results


def pack_places(out_ref, places_ref, exports_ref, counts_ref, side):
    base = NH * BA
    out_ref[base : base + 8, :] = jnp.zeros((8, out_ref.shape[1]), f32)
    for s in range(NH):
        chosen = exports_ref[0, side, s]
        lane = side * base + s * BA
        found = places_ref[:, :BA]
        for b in range(1, NB):
            found = jnp.where(chosen == b, places_ref[:, b * BA : (b + 1) * BA], found)
        out_ref[base : base + 3, lane : lane + BA] = found
        live = jnp.where(s < counts_ref[0, side], 1.0, 0.0)
        out_ref[base + 3 : base + 4, lane : lane + BA] = jnp.full((1, BA), live, f32)


def pack_rows(out_ref, rows_ref, exports_ref, side):
    for s in range(NH):
        start = pl.multiple_of(exports_ref[0, side, s] * BA, BA)
        out_ref[s * BA : (s + 1) * BA, :] = rows_ref[pl.ds(start, BA), :]


def head_kernel(
    features_ref, places_ref, charge_ref, anchor_ref, exports_ref, counts_ref,
    up_ref, down_ref, payload_ref,
    staged,
):
    for out_ref, side in ((up_ref, 0), (down_ref, 1)):
        pack_rows(out_ref, features_ref, exports_ref, side)
        pack_places(out_ref, places_ref, exports_ref, counts_ref, side)
    width = charge_ref.shape[0]
    charge_rows = jnp.transpose(
        jnp.concatenate([charge_ref[...], jnp.zeros((width, 6), f32)], axis=1)
    )
    charges = product(split(charge_rows), split(features_ref[...]), NT)
    chunks = features_ref.shape[0] // LANES
    for t in range(chunks):
        lane = slice(t * LANES, (t + 1) * LANES)
        for c in range(2):
            staged[c * chunks + t : c * chunks + t + 1, :] = charges[c : c + 1, lane]
        for d in range(3):
            row = (2 + d) * chunks + t
            staged[row : row + 1, :] = places_ref[d : d + 1, lane]
    anchors = anchor_ref[...].astype(f32)
    block = lanes_iota((3, LANES)) % (NB * BZ) // BZ
    spread = jnp.broadcast_to(anchors[:, :1], (3, LANES))
    for b in range(1, NB):
        spread = jnp.where(block == b, anchors[:, b : b + 1], spread)
    staged[5 * chunks : 5 * chunks + 3, :] = spread
    lane = lanes_iota((1, LANES))
    listed = jnp.zeros((1, LANES), jnp.int32)
    for side in range(2):
        for s in range(NH):
            listed = jnp.where(lane == side * NH + s, exports_ref[0, side, s], listed)
    staged[5 * chunks + 3 :, :] = listed.astype(f32)
    payload = staged[...]

    @pl.loop(0, payload_ref.shape[0])
    def _(domain):
        payload_ref[domain] = payload


def pair_terms(squared, live):
    softened = squared + soften
    near = jnp.exp(-2.0 * softened)
    if live is not None:
        near = near * live
    return near, jnp.exp(STEP * jnp.sqrt(softened))


def squared_distance(columns, rows):
    total = None
    for d in range(3):
        delta = columns[:, d : d + 1] - rows[d : d + 1, :]
        total = delta * delta if total is None else total + delta * delta
    return total


def scaled_weights(weight_ref):
    return [weight_ref[k : k + 1, :] * float(FACTORS[k]) for k in range(NR)]


def place_columns(places_ref):
    atoms = places_ref.shape[1]
    return jnp.transpose(jnp.concatenate([places_ref[...], jnp.zeros((5, atoms), f32)], axis=0))


def ghost_messages(ghost_values_ref, places_ref, ghost_places, weight_ref, out_ref):
    weights = scaled_weights(weight_ref)
    ghosts = 2 * NH * BA
    near, ratio = pair_terms(
        squared_distance(place_columns(places_ref), ghost_places[:, :ghosts]),
        ghost_places[3:4, :ghosts],
    )
    term = near

    def operands(k):
        nonlocal term
        after = term * ratio
        left = split(jnp.concatenate([term, after], axis=1))
        term = after * ratio
        values = ghost_values_ref[...]
        return left, split(
            jnp.concatenate([values * weights[k], values * weights[k + 1]], axis=0)
        )

    total = out_ref[...]
    ready = operands(0)
    for k in range(0, NR, 2):
        following = operands(k + 2) if k + 2 < NR else None
        total = total + product(*ready)
        ready = following
    out_ref[...] = total


def own_messages(values_ref, places_ref, weight_ref, out_ref):
    weights = scaled_weights(weight_ref)
    atoms = values_ref.shape[0]
    columns = place_columns(places_ref)
    half = lanes_iota((BA, 2 * BA)) >= BA
    partner = lanes_iota((BA, 2 * BA)) % BA
    other = (partner != rows_iota((BA, 2 * BA))).astype(f32)

    def one_block(b):
        rows = slice(b * BA, (b + 1) * BA)
        here = places_ref[:, rows]
        near, ratio = pair_terms(
            squared_distance(columns[rows], jnp.concatenate([here, here], axis=1)), other
        )
        term = jnp.where(half, near * ratio, near)
        ratio = ratio * ratio
        lefts, rights = [], []
        values = values_ref[rows, :]
        for k in range(0, NR, 2):
            lefts.append(term)
            rights.append(values * weights[k])
            rights.append(values * weights[k + 1])
            term = term * ratio
        left = split(jnp.concatenate(lefts, axis=1))
        right = split(jnp.concatenate(rights, axis=0))
        yield
        out_ref[rows, :] = product(left, right)

    blocks = atoms // BA
    for b in range(0, blocks, OWN_GROUP):
        side_by_side([one_block(b + n) for n in range(OWN_GROUP)])


def finish(hidden, messages, output_ref):
    scaled = messages * lax.rsqrt(
        jnp.mean(messages * messages, axis=-1, keepdims=True) + norm_epsilon
    )
    active = scaled / (1.0 + jnp.exp(-scaled))
    return hidden + product(split(active), split(output_ref[...]))


def first_own_kernel(features_ref, places_ref, value_one_ref, weight_ref, messages_ref, values):
    values[...] = product(split(features_ref[...]), split(value_one_ref[...]))
    own_messages(values, places_ref, weight_ref, messages_ref)


def first_layer_kernel(
    features_ref, own_ref, up_ref, down_ref, places_ref, value_one_ref, output_one_ref, weight_ref,
    value_two_ref, exports_ref,
    hidden_ref, values_two_ref, up_two_ref, down_two_ref, ghost_places_ref,
    ghost_values, messages,
):
    base = NH * BA
    ghost_rows = jnp.concatenate([up_ref[:base, :], down_ref[:base, :]], axis=0)
    ghost_values[...] = product(split(ghost_rows), split(value_one_ref[...]))
    ghost_places_ref[...] = up_ref[base : base + 8, :] + down_ref[base : base + 8, :]
    messages[...] = own_ref[...]
    ghost_messages(ghost_values, places_ref, ghost_places_ref[...], weight_ref, messages)
    hidden_ref[...] = finish(features_ref[...], messages[...], output_one_ref)
    values_two_ref[...] = product(split(hidden_ref[...]), split(value_two_ref[...]))
    pack_rows(up_two_ref, values_two_ref, exports_ref, 0)
    pack_rows(down_two_ref, values_two_ref, exports_ref, 1)


def second_layer_kernel(
    values_ref, up_two_ref, down_two_ref, ghost_places_ref, places_ref, weight_ref,
    return_ref, value_two_ref,
    messages_ref, returned_ref,
    ghost_values,
):
    base = NH * BA
    ghost_values[:base, :] = up_two_ref[...]
    ghost_values[base:, :] = down_two_ref[...]
    own_messages(values_ref, places_ref, weight_ref, messages_ref)
    ghost_messages(ghost_values, places_ref, ghost_places_ref[...], weight_ref, messages_ref)
    return_rows = jnp.concatenate(
        [return_ref[...], jnp.zeros((6, return_ref.shape[1]), f32)], axis=0
    )
    returned_ref[...] = product(split(return_rows), split(value_two_ref[...]))


def tail_kernel(
    received_ref, messages_ref, hidden_ref, ghost_places_ref, places_ref, weight_ref,
    return_ref, returned_ref, output_two_ref,
    updated_ref,
):
    atoms = hidden_ref.shape[0]
    ghosts = 2 * NH * BA
    potentials = jnp.sum(received_ref[...], axis=0)
    columns = jnp.transpose(potentials)
    ghost_places = ghost_places_ref[...]
    ghost_columns = jnp.transpose(ghost_places[:, :ghosts])
    own_columns = jnp.transpose(
        jnp.concatenate([places_ref[...], jnp.zeros((5, atoms), f32)], axis=0)
    )
    half = lanes_iota((BA, LANES)) >= BA
    other = (lanes_iota((BA, LANES)) % BA != rows_iota((BA, LANES))).astype(f32)
    ghost_potential = [
        jnp.concatenate([columns[c * BA : (c + 1) * BA, NB + s : NB + s + 1] for s in range(2 * NH)], axis=0)
        for c in range(2)
    ]
    pieces = []
    for t in range(atoms // LANES):
        lane = slice(t * LANES, (t + 1) * LANES)
        here = places_ref[:, lane]
        near, ratio = pair_terms(squared_distance(ghost_columns, here), ghost_columns[:, 3:4])
        squared = None
        own_potential = []
        for c in range(2):
            own_potential.append(
                jnp.where(
                    half,
                    columns[c * BA : (c + 1) * BA, 2 * t + 1 : 2 * t + 2],
                    columns[c * BA : (c + 1) * BA, 2 * t : 2 * t + 1],
                )
            )
        for d in range(3):
            first = own_columns[2 * t * BA : (2 * t + 1) * BA, d : d + 1]
            second = own_columns[(2 * t + 1) * BA : (2 * t + 2) * BA, d : d + 1]
            delta = jnp.where(half, second, first) - here[d : d + 1, :]
            squared = delta * delta if squared is None else squared + delta * delta
        own_near, own_ratio = pair_terms(squared, other)
        ratio = jnp.concatenate([ratio, own_ratio], axis=0)
        terms = [
            jnp.concatenate([near * ghost_potential[c], own_near * own_potential[c]], axis=0)
            for c in range(2)
        ]
        sums = []
        for k in range(NR):
            for c in range(2):
                sums.append(jnp.sum(terms[c], axis=0, keepdims=True))
                if k + 1 < NR:
                    terms[c] = terms[c] * ratio
        pieces.append(jnp.concatenate(sums, axis=0))
    gathered = jnp.transpose(jnp.concatenate(pieces, axis=1))
    spread = jnp.concatenate(
        [
            returned_ref[c : c + 1, :] * (weight_ref[k : k + 1, :] * float(FACTORS[k]))
            for k in range(NR)
            for c in range(2)
        ],
        axis=0,
    )
    messages = messages_ref[...] + narrow_product(split(gathered), split(spread))
    back = [return_ref[c : c + 1, :] for c in range(2)]
    layer_input = jnp.concatenate(
        [
            hidden_ref[b * BA : (b + 1) * BA, :]
            + columns[:BA, b : b + 1] * back[0]
            + columns[BA:, b : b + 1] * back[1]
            for b in range(atoms // BA)
        ],
        axis=0,
    )
    updated_ref[...] = finish(layer_input, messages, output_two_ref)


def transform_tables(grid):
    half = grid // 2
    u = np.arange(grid)
    x = np.concatenate([np.arange(half + 1), np.arange(1, half)])
    angle = 2.0 * np.pi * (np.outer(u, x) % grid) / grid
    table = np.where(np.arange(grid)[None] <= half, np.cos(angle), np.sin(angle)).astype(np.float32)
    back = (table.T / float(grid) ** 3).astype(np.float32)

    def halves(value):
        high = value.astype(bf16)
        low = (value - high.astype(np.float32)).astype(bf16)
        return np.concatenate([high, high, low], axis=1)

    return halves(table), halves(back)


def reciprocal_kernel(
    grid, slabs, per_slab, second, depth,
    place_ref, exports_ref, payload_ref, green_ref, forward_ref, back_ref,
    out_ref,
    planes_real, planes_imag, turns_high, turns_low, brick, carry,
    shift_cos, shift_sin, stage_cos, stage_sin, chosen, potential,
):
    planes = (planes_real, planes_imag)
    domains = slabs * per_slab
    half = grid // 2
    pitch = grid + 8
    thick = grid // slabs
    starts = thick - BX + 1
    rows = 2 * second
    cells = per_slab * NB * BZ
    atoms = per_slab * NB * BA
    chunks = atoms // LANES
    own = NB * BA // LANES
    wide = depth
    first_v = (place_ref[0] * second).astype(f32)
    first_w = (place_ref[1] * place_ref[2]).astype(f32)
    period = float(grid)

    row = rows_iota((rows, 1))
    frequency = jnp.where(row >= second, row - second, row).astype(f32) + first_v
    cosine, sine = wave(jnp.broadcast_to(frequency, (rows, LANES)), period)
    shift_cos[...] = cosine
    shift_sin[...] = sine
    upper = rows_iota((rows, LANES)) >= second
    carry[...] = jnp.zeros(carry.shape, f32)
    left_half = lanes_iota((1, LANES)) < LANES // 2

    def atom_rows(slab, t):
        base = slab * per_slab + t // own
        return [payload_ref[base, q * own + t % own : q * own + t % own + 1, :] for q in range(5)]

    def windows(parts):
        cell = rows_iota((BY, LANES)).astype(f32)
        along_x = [jnp.exp(-((float(i) - parts[2] * 1.5) ** 2)) for i in range(BX)]
        along_y = jnp.exp(-((cell - parts[3] * 3.5) ** 2))
        along_z = jnp.exp(-((cell - parts[4] * 3.5) ** 2))
        return along_x, along_y, along_z

    def anchor(slab, dim):
        found = []
        for q in range(0, per_slab, 2):
            one = payload_ref[slab * per_slab + q, 5 * own + dim : 5 * own + dim + 1, :]
            two = payload_ref[slab * per_slab + q + 1, 5 * own + dim : 5 * own + dim + 1, :]
            found.append(jnp.where(left_half, one, two))
        return jnp.concatenate(found, axis=1) if len(found) > 1 else found[0]

    def spread_of(slab):
        both, pieces = [], []
        for t in range(chunks):
            parts = atom_rows(slab, t)
            along = windows(parts)
            pieces.append(jnp.where(left_half, along[2], 0.0))
            pieces.append(jnp.where(left_half, 0.0, along[2]))
            both.append((parts, along))
        return both, split(jnp.concatenate(pieces, axis=0))

    piece_of = lanes_iota((1, cells)) // (2 * BZ)

    def slab_masks(slab):
        start = anchor(slab, 0) - (slab * thick).astype(f32)
        return [(start == float(s)).astype(f32) for s in range(starts)]

    def deposit(slab, side):
        both, spread = spread_of(slab)
        lefts = []
        for parts, (along_x, along_y, _) in both:
            for c in range(2):
                for i in range(BX):
                    lefts.append((parts[c] * along_x[i]) * along_y)
        operand = split(jnp.concatenate(lefts, axis=0))
        yield
        found = product(operand, spread, NT)
        yield
        height = 2 * BX * BY
        total = found[:height]
        for t in range(1, chunks):
            total = jnp.where(piece_of == t, found[t * height : (t + 1) * height], total)
        brick[side] = total
        low_cell = anchor(slab, 2) + (lanes_iota((1, cells)) % BZ).astype(f32)
        ramp = rows_iota((8, cells)).astype(f32) + first_w
        cosine, sine = wave(ramp * low_cell, period)
        turn_cos, turn_sin = wave(8.0 * low_cell, period)
        for g in range(wide // 8):
            at = slice(g * 8, (g + 1) * 8)
            stage_cos[side, at, :] = cosine
            stage_sin[side, at, :] = sine
            cosine, sine = cosine * turn_cos - sine * turn_sin, cosine * turn_sin + sine * turn_cos
        cos_high, cos_low = split(stage_cos[side])
        sin_high, sin_low = split(stage_sin[side])
        for ref, c_part, s_part in ((turns_high, cos_high, sin_high), (turns_low, cos_low, sin_low)):
            ref[slab, :wide, :cells] = c_part
            ref[slab, :wide, cells:] = s_part
            ref[slab, wide:, :cells] = -s_part
            ref[slab, wide:, cells:] = c_part
        wide_cos = jnp.concatenate([shift_cos[...]] * (cells // LANES), axis=1)
        wide_sin = jnp.concatenate([shift_sin[...]] * (cells // LANES), axis=1)
        top = jnp.concatenate([upper] * (cells // LANES), axis=1) if cells > LANES else upper
        cosine, sine = wave(frequency * anchor(slab, 1), period)
        real = [jnp.zeros((rows, cells), f32)] * BX
        imag = [jnp.zeros((rows, cells), f32)] * BX
        for j in range(BY):
            for i in range(BX):
                low = brick[side, i * BY + j : i * BY + j + 1, :]
                high = brick[side, (BX + i) * BY + j : (BX + i) * BY + j + 1, :]
                weight = jnp.where(top, high, low)
                real[i] = real[i] + weight * cosine
                imag[i] = imag[i] - weight * sine
            if j + 1 < BY:
                cosine, sine = (
                    cosine * wide_cos - sine * wide_sin,
                    cosine * wide_sin + sine * wide_cos,
                )
        masks = slab_masks(slab)
        placed = []
        for x in range(thick):
            parts = []
            for source in (real, imag):
                total = None
                for i in range(BX):
                    if 0 <= x - i < starts:
                        piece = source[i] * masks[x - i]
                        total = piece if total is None else total + piece
                parts.append(total)
            placed.append(jnp.concatenate(parts, axis=1))
        operand = split(jnp.concatenate(placed, axis=0))
        yield
        return product(operand, (turns_high[slab], turns_low[slab]), NT)

    def put(x, value):
        for part, ref in enumerate(planes):
            ref[pl.ds(x, rows, stride=pitch), :] = value[:, part * wide : (part + 1) * wide]

    def get(x):
        return jnp.concatenate([ref[pl.ds(x, rows, stride=pitch), :] for ref in planes], axis=1)

    def swapped(value):
        return jnp.concatenate([value[:, wide:], -value[:, :wide]], axis=1)

    pairs = 2 if slabs % 4 == 0 else 1

    @pl.loop(0, slabs // 2 // pairs)
    def _(step):
        first = [step * pairs + n for n in range(pairs)]
        both = [slab for m in first for slab in (m, slabs - 1 - m)]
        found = side_by_side([deposit(slab, side) for side, slab in enumerate(both)])
        last = carry[...]
        for n, m in enumerate(first):
            near, far = found[2 * n], found[2 * n + 1]
            for r in range(thick):
                x = m * thick + r
                one = near[r * rows : (r + 1) * rows]
                two = last if r == 0 else far[(thick - r) * rows : (thick - r + 1) * rows]
                put(x, one + two)
                put(half + x, swapped(one - two))
            last = far[:rows]
        carry[...] = last

    put(half, carry[...])

    def padded(kernel):
        gap = wide - kernel.shape[1]
        if gap == 0:
            return kernel
        return jnp.concatenate([kernel, jnp.zeros((kernel.shape[0], gap), f32)], axis=1)

    def transformed(table_ref, value):
        high, low = split(value)
        return lax.dot_general(
            table_ref[...], jnp.concatenate([high, low, high], axis=0), NN, preferred_element_type=f32
        )

    together = 2 if second % 2 == 0 else 1

    @pl.loop(0, second // together)
    def _(step):
        frequencies = [step * together + n for n in range(together)]
        places = [
            pl.ds(pl.multiple_of((c * second + v) * pitch, 8), grid)
            for v in frequencies
            for c in range(2)
        ]
        inside = jnp.concatenate([ref[place, :] for place in places for ref in planes], axis=1)
        spectrum = transformed(forward_ref, inside)
        outside = []
        for n, v in enumerate(frequencies):
            for c in range(2):
                zero, one = padded(green_ref[v, c, 0]), padded(green_ref[v, c, 1])
                for part in range(2):
                    at = (4 * n + part) * wide
                    outside.append(
                        zero * spectrum[:, at : at + wide]
                        + one * spectrum[:, at + 2 * wide : at + 3 * wide]
                    )
        result = transformed(back_ref, jnp.concatenate(outside, axis=1))
        for n, place in enumerate(places):
            for part, ref in enumerate(planes):
                at = (2 * n + part) * wide
                ref[place, :] = result[:, at : at + wide]

    def evaluate(slab, inputs, side):
        masks = slab_masks(slab)
        both, spread = spread_of(slab)
        operand = split(jnp.concatenate(inputs, axis=0))
        yield
        found = product(operand, (turns_high[slab], turns_low[slab]))
        yield
        twice = [jnp.concatenate([mask, mask], axis=1) for mask in masks]
        for i in range(BX):
            total = None
            for s in range(starts):
                piece = found[(s + i) * rows : (s + i + 1) * rows] * twice[s]
                total = piece if total is None else total + piece
            chosen[side, i * rows : (i + 1) * rows, :] = total
        cell = anchor(slab, 1) + rows_iota((BY, cells)).astype(f32)
        cosine, sine = wave(cell * first_v, period)
        turn_cos, turn_sin = wave(cell, period)
        sums = [jnp.zeros((BY, cells), f32)] * (2 * BX)
        for v in range(second):
            for c in range(2):
                for i in range(BX):
                    at = i * rows + c * second + v
                    sums[c * BX + i] = (
                        sums[c * BX + i]
                        + chosen[side, at : at + 1, :cells] * cosine
                        - chosen[side, at : at + 1, cells:] * sine
                    )
            if v + 1 < second:
                cosine, sine = cosine * turn_cos - sine * turn_sin, cosine * turn_sin + sine * turn_cos
        summed = jnp.concatenate(sums, axis=0)
        masked = [jnp.where(piece_of == t, summed, 0.0) for t in range(chunks)]
        operand = split(jnp.concatenate(masked, axis=0))
        yield
        at_atoms = product(operand, spread)
        yield
        for t in range(chunks):
            _, (along_x, along_y, _) = both[t]
            pair = []
            for c in range(2):
                total = None
                for i in range(BX):
                    at = (t * 2 * BX + c * BX + i) * BY
                    piece = at_atoms[at : at + BY] * along_x[i]
                    total = piece if total is None else total + piece
                pair.append(jnp.sum(total * along_y, axis=0, keepdims=True))
            one = jnp.where(left_half, pair[0], pltpu.roll(pair[1], LANES // 2, 1))
            two = jnp.where(left_half, pltpu.roll(pair[0], LANES // 2, 1), pair[1])
            potential[pl.ds(slab * per_slab * NB + 2 * t, 1), :] = one
            potential[pl.ds(slab * per_slab * NB + 2 * t + 1, 1), :] = two

    def straight(x):
        even = get(x)
        odd = get(jnp.minimum(half + x, grid - 1)) * jnp.where((x > 0) & (x < half), 1.0, 0.0)
        turned = jnp.concatenate([-odd[:, wide:], odd[:, :wide]], axis=1)
        return even + turned, even - turned

    @pl.loop(0, slabs // 2 // pairs)
    def _(step):
        works = []
        for n in range(pairs):
            m = step * pairs + n
            near, far = [], [None] * thick
            for r in range(thick):
                ahead, behind = straight(m * thick + r)
                near.append(ahead)
                if r > 0:
                    far[thick - r] = behind
            far[0] = straight(m * thick + thick)[1]
            works.append(evaluate(m, near, 2 * n))
            works.append(evaluate(slabs - 1 - m, far, 2 * n + 1))
        side_by_side(works)

    @pl.loop(0, domains)
    def _(domain):
        out_ref[domain, NB + 2 * NH :, :] = jnp.zeros((16 - NB - 2 * NH, LANES), f32)
        out_ref[domain, :NB, :] = potential[pl.ds(pl.multiple_of(domain * NB, NB), NB), :]
        below = lax.rem(domain + domains - 1, domains)
        above = lax.rem(domain + 1, domains)
        for s in range(NH):
            at = below * NB + exports_ref[below, s]
            out_ref[domain, NB + s : NB + s + 1, :] = potential[pl.ds(at, 1), :]
            at = above * NB + exports_ref[above, NH + s]
            out_ref[domain, NB + NH + s : NB + NH + s + 1, :] = potential[pl.ds(at, 1), :]


def build_reciprocal(grid, slabs, per_slab, second, depth):
    domains = slabs * per_slab
    cells = per_slab * NB * BZ
    return pl.pallas_call(
        functools.partial(reciprocal_kernel, grid, slabs, per_slab, second, depth),
        in_specs=[SMEM, SMEM] + [VMEM] * 4,
        out_specs=VMEM,
        out_shape=jax.ShapeDtypeStruct((domains, 16, LANES), f32),
        scratch_shapes=[
            pltpu.VMEM((2 * second * (grid + 8), depth), f32),
            pltpu.VMEM((2 * second * (grid + 8), depth), f32),
            pltpu.VMEM((slabs, 2 * depth, 2 * cells), bf16),
            pltpu.VMEM((slabs, 2 * depth, 2 * cells), bf16),
            pltpu.VMEM((4, 2 * BX * BY, cells), f32),
            pltpu.VMEM((2 * second, 2 * depth), f32),
            pltpu.VMEM((2 * second, LANES), f32),
            pltpu.VMEM((2 * second, LANES), f32),
            pltpu.VMEM((4, depth, cells), f32),
            pltpu.VMEM((4, depth, cells), f32),
            pltpu.VMEM((4, BX * 2 * second, 2 * cells), f32),
            pltpu.VMEM((domains * NB, LANES), f32),
        ],
        compiler_params=params(),
    )


VMEM = pl.BlockSpec(memory_space=pltpu.VMEM)
SMEM = pl.BlockSpec(memory_space=pltpu.SMEM)


def per_device(
    features,
    positions,
    value_one,
    output_one,
    radial_one,
    value_two,
    output_two,
    radial_two,
    charge_weight,
    return_weight,
    green_kernel,
    exports,
    export_counts,
    brick_anchor,
):
    axes = ("dom", "rec")
    slabs, per_slab = lax.axis_size("dom"), lax.axis_size("rec")
    domains = slabs * per_slab
    atoms, width = features.shape
    depth_rows, grid, second = green_kernel.shape[0], green_kernel.shape[3], green_kernel.shape[4]
    depth = -(-depth_rows // LANES) * LANES
    chunks = atoms // LANES
    payload_rows = 5 * chunks + 4
    base = NH * BA

    def shape(*dims):
        return jax.ShapeDtypeStruct(dims, f32)

    def around(rows, by):
        return lax.ppermute(rows, axes, [(i, (i + by) % domains) for i in range(domains)])

    up, down, payload = pl.pallas_call(
        head_kernel,
        in_specs=[VMEM] * 4 + [SMEM] * 2,
        out_specs=[VMEM] * 3,
        out_shape=[
            shape(base + 8, width), shape(base + 8, width), shape(domains, payload_rows, LANES)
        ],
        scratch_shapes=[pltpu.VMEM((payload_rows, LANES), f32)],
        compiler_params=params(),
    )(features, positions, charge_weight, brick_anchor, exports, export_counts)

    everyone = lax.all_to_all(payload, axes, 0, 0, tiled=True)
    up, down, green_kernel, features = lax.optimization_barrier((up, down, green_kernel, features))
    up = around(up, 1)
    down = around(down, -1)
    green = jnp.transpose(green_kernel, (4, 1, 2, 3, 0))
    own = pl.pallas_call(
        first_own_kernel,
        in_specs=[VMEM] * 4,
        out_specs=VMEM,
        out_shape=shape(atoms, width),
        scratch_shapes=[pltpu.VMEM((atoms, width), f32)],
        compiler_params=params(),
    )(features, positions, value_one, radial_one)
    own, green, up, down = lax.optimization_barrier((own, green, up, down))

    hidden, values_two, up_two, down_two, ghost_places = pl.pallas_call(
        first_layer_kernel,
        in_specs=[VMEM] * 9 + [SMEM],
        out_specs=[VMEM] * 5,
        out_shape=[
            shape(atoms, width), shape(atoms, width), shape(base, width), shape(base, width),
            shape(8, width),
        ],
        scratch_shapes=[
            pltpu.VMEM((2 * base, width), f32),
            pltpu.VMEM((atoms, width), f32),
        ],
        compiler_params=params(),
    )(features, own, up, down, positions, value_one, output_one, radial_one, value_two, exports)

    everyone, hidden = lax.optimization_barrier((everyone, hidden))
    up_two = around(up_two, 1)
    down_two = around(down_two, -1)

    place = jnp.stack(
        [lax.axis_index("dom"), lax.axis_index("rec"), jnp.int32(depth_rows)]
    ).astype(jnp.int32)
    all_exports = everyone[:, 5 * chunks + 3, :8].astype(jnp.int32)
    table, table_back = transform_tables(grid)
    outgoing = build_reciprocal(grid, slabs, per_slab, second, depth)(
        place, all_exports, everyone, green, table, table_back
    )

    outgoing, up_two, down_two = lax.optimization_barrier((outgoing, up_two, down_two))
    received = lax.all_to_all(outgoing, axes, 0, 0, tiled=True)

    messages, returned = pl.pallas_call(
        second_layer_kernel,
        in_specs=[VMEM] * 8,
        out_specs=[VMEM] * 2,
        out_shape=[shape(atoms, width), shape(8, width)],
        scratch_shapes=[pltpu.VMEM((2 * base, width), f32)],
        compiler_params=params(),
    )(values_two, up_two, down_two, ghost_places, positions, radial_two, return_weight, value_two)

    return pl.pallas_call(
        tail_kernel,
        in_specs=[VMEM] * 9,
        out_specs=VMEM,
        out_shape=shape(atoms, width),
        compiler_params=params(),
    )(
        received, messages, hidden, ghost_places, positions, radial_two, return_weight, returned, output_two
    )


def solution(mesh):
    placed = (
        P(("dom", "rec"), None),
        P(None, ("dom", "rec")),
        P(),
        P(),
        P(),
        P(),
        P(),
        P(),
        P(),
        P(),
        P("rec", None, None, None, "dom"),
        P(("dom", "rec"), None, None),
        P(("dom", "rec"), None),
        P(None, ("dom", "rec")),
    )
    return jax.shard_map(
        per_device, mesh=mesh, in_specs=placed, out_specs=P(("dom", "rec"), None), check_vma=False
    )
```

```python
import functools
import math

import jax
import jax.numpy as jnp
import numpy as np
from jax import lax
from jax.experimental import pallas as pl
from jax.experimental.pallas import tpu as pltpu
from jax.sharding import PartitionSpec as P

BA = 64
BX = 4
BY = 8
BZ = 8
NB = 8
NH = 3
NR = 8
LANES = 128

soften = 0.01
norm_epsilon = 1e-05
f32 = jnp.float32
bf16 = jnp.bfloat16
NN = (((1,), (0,)), ((), ()))
NT = (((1,), (1,)), ((), ()))
STEP = 12.0 / 7.0
OWN_GROUP = 4
FACTORS = np.exp(-18.0 * np.arange(NR) ** 2 / 49.0).astype(np.float32)


def params(mib=60):
    return pltpu.CompilerParams(vmem_limit_bytes=mib * 1024 * 1024)


def split(value):
    high = value.astype(bf16)
    return high, (value - high.astype(f32)).astype(bf16)


def product(left, right, dims=NN):
    axis = dims[0][1][0]
    return lax.dot_general(
        jnp.concatenate([left[0], left[0], left[1]], axis=1),
        jnp.concatenate([right[0], right[1], right[0]], axis=axis),
        dims,
        preferred_element_type=f32,
    )


def narrow_product(left, right):
    def one(a, b):
        return lax.dot_general(a, b, NN, preferred_element_type=f32)

    return one(left[0], right[0]) + (one(left[0], right[1]) + one(left[1], right[0]))


def wave(phase, period):
    rest = phase - period * jnp.floor(phase * (1.0 / period) + 0.5)
    turn = rest * (1.0 / period)
    square = turn * turn
    cosine = jnp.full_like(turn, (-1) ** 9 * (2 * math.pi) ** 18 / math.factorial(18))
    sine = jnp.full_like(turn, (-1) ** 9 * (2 * math.pi) ** 19 / math.factorial(19))
    for n in range(8, -1, -1):
        cosine = cosine * square + (-1) ** n * (2 * math.pi) ** (2 * n) / math.factorial(2 * n)
        sine = sine * square + (-1) ** n * (2 * math.pi) ** (2 * n + 1) / math.factorial(2 * n + 1)
    return cosine, sine * turn


def rows_iota(shape):
    return lax.broadcasted_iota(jnp.int32, shape, len(shape) - 2)


def lanes_iota(shape):
    return lax.broadcasted_iota(jnp.int32, shape, len(shape) - 1)


def side_by_side(works):
    results = [None] * len(works)
    waiting = list(range(len(works)))
    while waiting:
        for n in list(waiting):
            try:
                next(works[n])
            except StopIteration as end:
                results[n] = end.value
                waiting.remove(n)
    return results


def pack_places(out_ref, places_ref, exports_ref, counts_ref, side):
    base = NH * BA
    out_ref[base : base + 8, :] = jnp.zeros((8, out_ref.shape[1]), f32)
    for s in range(NH):
        chosen = exports_ref[0, side, s]
        lane = side * base + s * BA
        found = places_ref[:, :BA]
        for b in range(1, NB):
            found = jnp.where(chosen == b, places_ref[:, b * BA : (b + 1) * BA], found)
        out_ref[base : base + 3, lane : lane + BA] = found
        live = jnp.where(s < counts_ref[0, side], 1.0, 0.0)
        out_ref[base + 3 : base + 4, lane : lane + BA] = jnp.full((1, BA), live, f32)


def pack_rows(out_ref, rows_ref, exports_ref, side):
    for s in range(NH):
        start = pl.multiple_of(exports_ref[0, side, s] * BA, BA)
        out_ref[s * BA : (s + 1) * BA, :] = rows_ref[pl.ds(start, BA), :]


def head_kernel(
    features_ref, places_ref, charge_ref, anchor_ref, exports_ref, counts_ref,
    up_ref, down_ref, payload_ref,
    staged,
):
    for out_ref, side in ((up_ref, 0), (down_ref, 1)):
        pack_rows(out_ref, features_ref, exports_ref, side)
        pack_places(out_ref, places_ref, exports_ref, counts_ref, side)
    charge_rows = jnp.concatenate(
        [charge_ref[...], jnp.zeros((6, charge_ref.shape[1]), f32)], axis=0
    )
    charges = product(split(charge_rows), split(features_ref[...]), NT)
    chunks = features_ref.shape[0] // LANES
    for t in range(chunks):
        lane = slice(t * LANES, (t + 1) * LANES)
        for c in range(2):
            staged[c * chunks + t : c * chunks + t + 1, :] = charges[c : c + 1, lane]
        for d in range(3):
            row = (2 + d) * chunks + t
            staged[row : row + 1, :] = places_ref[d : d + 1, lane]
    anchors = anchor_ref[...].astype(f32)
    block = lanes_iota((3, LANES)) % (NB * BZ) // BZ
    spread = jnp.broadcast_to(anchors[:, :1], (3, LANES))
    for b in range(1, NB):
        spread = jnp.where(block == b, anchors[:, b : b + 1], spread)
    staged[5 * chunks : 5 * chunks + 3, :] = spread
    lane = lanes_iota((1, LANES))
    listed = jnp.zeros((1, LANES), jnp.int32)
    for side in range(2):
        for s in range(NH):
            listed = jnp.where(lane == side * NH + s, exports_ref[0, side, s], listed)
    staged[5 * chunks + 3 :, :] = listed.astype(f32)
    payload = staged[...]

    @pl.loop(0, payload_ref.shape[0])
    def _(domain):
        payload_ref[domain] = payload


def pair_terms(squared, live):
    softened = squared + soften
    near = jnp.exp(-2.0 * softened)
    if live is not None:
        near = near * live
    return near, jnp.exp(STEP * (softened * lax.rsqrt(softened)))


def squared_distance(columns, rows):
    total = None
    for d in range(3):
        delta = columns[:, d : d + 1] - rows[d : d + 1, :]
        total = delta * delta if total is None else total + delta * delta
    return total


def scaled_weights(weight_ref):
    return [weight_ref[k : k + 1, :] * float(FACTORS[k]) for k in range(NR)]


def place_columns(places_ref):
    atoms = places_ref.shape[1]
    return jnp.transpose(jnp.concatenate([places_ref[...], jnp.zeros((5, atoms), f32)], axis=0))


def ghost_messages(ghost_values_ref, places_ref, ghost_places, weight_ref, out_ref):
    weights = scaled_weights(weight_ref)
    ghosts = 2 * NH * BA
    near, ratio = pair_terms(
        squared_distance(place_columns(places_ref), ghost_places[:, :ghosts]),
        ghost_places[3:4, :ghosts],
    )
    term = near

    def operands(k):
        nonlocal term
        after = term * ratio
        left = split(jnp.concatenate([term, after], axis=1))
        term = after * ratio
        values = ghost_values_ref[...]
        return left, split(
            jnp.concatenate([values * weights[k], values * weights[k + 1]], axis=0)
        )

    total = out_ref[...]
    ready = operands(0)
    for k in range(0, NR, 2):
        following = operands(k + 2) if k + 2 < NR else None
        total = total + product(*ready)
        ready = following
    out_ref[...] = total


def own_messages(values_ref, places_ref, weight_ref, out_ref):
    weights = scaled_weights(weight_ref)
    atoms = values_ref.shape[0]
    columns = place_columns(places_ref)
    half = lanes_iota((BA, 2 * BA)) >= BA
    partner = lanes_iota((BA, 2 * BA)) % BA
    other = (partner != rows_iota((BA, 2 * BA))).astype(f32)

    def one_block(b):
        rows = slice(b * BA, (b + 1) * BA)
        here = places_ref[:, rows]
        near, ratio = pair_terms(
            squared_distance(columns[rows], jnp.concatenate([here, here], axis=1)), other
        )
        term = jnp.where(half, near * ratio, near)
        ratio = ratio * ratio
        lefts, rights = [], []
        values = values_ref[rows, :]
        for k in range(0, NR, 2):
            lefts.append(term)
            rights.append(values * weights[k])
            rights.append(values * weights[k + 1])
            term = term * ratio
        left = split(jnp.concatenate(lefts, axis=1))
        right = split(jnp.concatenate(rights, axis=0))
        yield
        out_ref[rows, :] = product(left, right)

    blocks = atoms // BA
    for b in range(0, blocks, OWN_GROUP):
        side_by_side([one_block(b + n) for n in range(OWN_GROUP)])


def finish(hidden, messages, output_ref):
    scaled = messages * lax.rsqrt(
        jnp.mean(messages * messages, axis=-1, keepdims=True) + norm_epsilon
    )
    active = scaled / (1.0 + jnp.exp(-scaled))
    return hidden + product(split(active), split(output_ref[...]))


def first_own_kernel(features_ref, places_ref, value_one_ref, weight_ref, messages_ref, values):
    values[...] = product(split(features_ref[...]), split(value_one_ref[...]))
    own_messages(values, places_ref, weight_ref, messages_ref)


def first_layer_kernel(
    features_ref, own_ref, up_ref, down_ref, places_ref, value_one_ref, output_one_ref, weight_ref,
    value_two_ref, exports_ref,
    hidden_ref, values_two_ref, up_two_ref, down_two_ref, ghost_places_ref,
    ghost_values, messages,
):
    base = NH * BA
    ghost_rows = jnp.concatenate([up_ref[:base, :], down_ref[:base, :]], axis=0)
    ghost_values[...] = product(split(ghost_rows), split(value_one_ref[...]))
    ghost_places_ref[...] = up_ref[base : base + 8, :] + down_ref[base : base + 8, :]
    messages[...] = own_ref[...]
    ghost_messages(ghost_values, places_ref, ghost_places_ref[...], weight_ref, messages)
    hidden_ref[...] = finish(features_ref[...], messages[...], output_one_ref)
    values_two_ref[...] = product(split(hidden_ref[...]), split(value_two_ref[...]))
    pack_rows(up_two_ref, values_two_ref, exports_ref, 0)
    pack_rows(down_two_ref, values_two_ref, exports_ref, 1)


def second_layer_kernel(
    values_ref, up_two_ref, down_two_ref, ghost_places_ref, places_ref, weight_ref,
    return_ref, value_two_ref,
    messages_ref, returned_ref,
    ghost_values,
):
    base = NH * BA
    ghost_values[:base, :] = up_two_ref[...]
    ghost_values[base:, :] = down_two_ref[...]
    own_messages(values_ref, places_ref, weight_ref, messages_ref)
    ghost_messages(ghost_values, places_ref, ghost_places_ref[...], weight_ref, messages_ref)
    return_rows = jnp.concatenate(
        [return_ref[...], jnp.zeros((6, return_ref.shape[1]), f32)], axis=0
    )
    returned_ref[...] = product(split(return_rows), split(value_two_ref[...]))


def tail_kernel(
    received_ref, messages_ref, hidden_ref, ghost_places_ref, places_ref, weight_ref,
    return_ref, returned_ref, output_two_ref,
    updated_ref,
):
    atoms = hidden_ref.shape[0]
    ghosts = 2 * NH * BA
    potentials = jnp.sum(received_ref[...], axis=0)
    columns = jnp.transpose(potentials)
    ghost_places = ghost_places_ref[...]
    ghost_columns = jnp.transpose(ghost_places[:, :ghosts])
    own_columns = jnp.transpose(
        jnp.concatenate([places_ref[...], jnp.zeros((5, atoms), f32)], axis=0)
    )
    half = lanes_iota((BA, LANES)) >= BA
    other = (lanes_iota((BA, LANES)) % BA != rows_iota((BA, LANES))).astype(f32)
    ghost_potential = [
        jnp.concatenate([columns[c * BA : (c + 1) * BA, NB + s : NB + s + 1] for s in range(2 * NH)], axis=0)
        for c in range(2)
    ]
    pieces = []
    for t in range(atoms // LANES):
        lane = slice(t * LANES, (t + 1) * LANES)
        here = places_ref[:, lane]
        near, ratio = pair_terms(squared_distance(ghost_columns, here), ghost_columns[:, 3:4])
        squared = None
        own_potential = []
        for c in range(2):
            own_potential.append(
                jnp.where(
                    half,
                    columns[c * BA : (c + 1) * BA, 2 * t + 1 : 2 * t + 2],
                    columns[c * BA : (c + 1) * BA, 2 * t : 2 * t + 1],
                )
            )
        for d in range(3):
            first = own_columns[2 * t * BA : (2 * t + 1) * BA, d : d + 1]
            second = own_columns[(2 * t + 1) * BA : (2 * t + 2) * BA, d : d + 1]
            delta = jnp.where(half, second, first) - here[d : d + 1, :]
            squared = delta * delta if squared is None else squared + delta * delta
        own_near, own_ratio = pair_terms(squared, other)
        ratio = jnp.concatenate([ratio, own_ratio], axis=0)
        terms = [
            jnp.concatenate([near * ghost_potential[c], own_near * own_potential[c]], axis=0)
            for c in range(2)
        ]
        sums = []
        for k in range(NR):
            for c in range(2):
                sums.append(jnp.sum(terms[c], axis=0, keepdims=True))
                if k + 1 < NR:
                    terms[c] = terms[c] * ratio
        pieces.append(jnp.concatenate(sums, axis=0))
    gathered = jnp.transpose(jnp.concatenate(pieces, axis=1))
    spread = jnp.concatenate(
        [
            returned_ref[c : c + 1, :] * (weight_ref[k : k + 1, :] * float(FACTORS[k]))
            for k in range(NR)
            for c in range(2)
        ],
        axis=0,
    )
    messages = messages_ref[...] + narrow_product(split(gathered), split(spread))
    back = [return_ref[c : c + 1, :] for c in range(2)]
    layer_input = jnp.concatenate(
        [
            hidden_ref[b * BA : (b + 1) * BA, :]
            + columns[:BA, b : b + 1] * back[0]
            + columns[BA:, b : b + 1] * back[1]
            for b in range(atoms // BA)
        ],
        axis=0,
    )
    updated_ref[...] = finish(layer_input, messages, output_two_ref)


def transform_tables(grid):
    half = grid // 2
    u = np.arange(grid)
    x = np.concatenate([np.arange(half + 1), np.arange(1, half)])
    angle = 2.0 * np.pi * (np.outer(u, x) % grid) / grid
    table = np.where(np.arange(grid)[None] <= half, np.cos(angle), np.sin(angle)).astype(np.float32)
    back = (table.T / float(grid) ** 3).astype(np.float32)

    def halves(value):
        high = value.astype(bf16)
        low = (value - high.astype(np.float32)).astype(bf16)
        return np.concatenate([high, high, low], axis=1)

    return halves(table), halves(back)


def reciprocal_kernel(
    grid, slabs, per_slab, second, depth,
    place_ref, exports_ref, payload_ref, green_hbm, forward_ref, back_ref,
    out_ref,
    green_ref, green_arrived, planes_real, planes_imag, turns_high, turns_low, brick, carry,
    shift_cos, shift_sin, stage_cos, stage_sin, chosen, potential,
):
    green_copy = pltpu.make_async_copy(green_hbm, green_ref, green_arrived)
    green_copy.start()
    planes = (planes_real, planes_imag)
    domains = slabs * per_slab
    half = grid // 2
    pitch = grid + 8
    thick = grid // slabs
    starts = thick - BX + 1
    rows = 2 * second
    cells = per_slab * NB * BZ
    atoms = per_slab * NB * BA
    chunks = atoms // LANES
    own = NB * BA // LANES
    wide = depth
    first_v = (place_ref[0] * second).astype(f32)
    first_w = (place_ref[1] * place_ref[2]).astype(f32)
    period = float(grid)

    row = rows_iota((rows, 1))
    frequency = jnp.where(row >= second, row - second, row).astype(f32) + first_v
    cosine, sine = wave(jnp.broadcast_to(frequency, (rows, LANES)), period)
    shift_cos[...] = cosine
    shift_sin[...] = sine
    upper = rows_iota((rows, LANES)) >= second
    carry[...] = jnp.zeros(carry.shape, f32)
    left_half = lanes_iota((1, LANES)) < LANES // 2

    def atom_rows(slab, t):
        base = slab * per_slab + t // own
        return [payload_ref[base, q * own + t % own : q * own + t % own + 1, :] for q in range(5)]

    def windows(parts):
        cell = rows_iota((BY, LANES)).astype(f32)
        along_x = [jnp.exp(-((float(i) - parts[2] * 1.5) ** 2)) for i in range(BX)]
        along_y = jnp.exp(-((cell - parts[3] * 3.5) ** 2))
        along_z = jnp.exp(-((cell - parts[4] * 3.5) ** 2))
        return along_x, along_y, along_z

    def anchor(slab, dim):
        found = []
        for q in range(0, per_slab, 2):
            one = payload_ref[slab * per_slab + q, 5 * own + dim : 5 * own + dim + 1, :]
            two = payload_ref[slab * per_slab + q + 1, 5 * own + dim : 5 * own + dim + 1, :]
            found.append(jnp.where(left_half, one, two))
        return jnp.concatenate(found, axis=1) if len(found) > 1 else found[0]

    def spread_of(slab):
        both, pieces = [], []
        for t in range(chunks):
            parts = atom_rows(slab, t)
            along = windows(parts)
            pieces.append(jnp.where(left_half, along[2], 0.0))
            pieces.append(jnp.where(left_half, 0.0, along[2]))
            both.append((parts, along))
        return both, split(jnp.concatenate(pieces, axis=0))

    piece_of = lanes_iota((1, cells)) // (2 * BZ)

    def slab_masks(slab):
        start = anchor(slab, 0) - (slab * thick).astype(f32)
        return [(start == float(s)).astype(f32) for s in range(starts)]

    def deposit(slab, side):
        both, spread = spread_of(slab)
        lefts = []
        for parts, (along_x, along_y, _) in both:
            for c in range(2):
                for i in range(BX):
                    lefts.append((parts[c] * along_x[i]) * along_y)
        operand = split(jnp.concatenate(lefts, axis=0))
        yield
        found = product(operand, spread, NT)
        yield
        height = 2 * BX * BY
        total = found[:height]
        for t in range(1, chunks):
            total = jnp.where(piece_of == t, found[t * height : (t + 1) * height], total)
        brick[side] = total
        low_cell = anchor(slab, 2) + (lanes_iota((1, cells)) % BZ).astype(f32)
        ramp = rows_iota((8, cells)).astype(f32) + first_w
        cosine, sine = wave(ramp * low_cell, period)
        turn_cos, turn_sin = wave(8.0 * low_cell, period)
        for g in range(wide // 8):
            at = slice(g * 8, (g + 1) * 8)
            stage_cos[side, at, :] = cosine
            stage_sin[side, at, :] = sine
            cosine, sine = cosine * turn_cos - sine * turn_sin, cosine * turn_sin + sine * turn_cos
        cos_high, cos_low = split(stage_cos[side])
        sin_high, sin_low = split(stage_sin[side])
        for ref, c_part, s_part in ((turns_high, cos_high, sin_high), (turns_low, cos_low, sin_low)):
            ref[slab, :wide, :cells] = c_part
            ref[slab, :wide, cells:] = s_part
            ref[slab, wide:, :cells] = -s_part
            ref[slab, wide:, cells:] = c_part
        wide_cos = jnp.concatenate([shift_cos[...]] * (cells // LANES), axis=1)
        wide_sin = jnp.concatenate([shift_sin[...]] * (cells // LANES), axis=1)
        top = jnp.concatenate([upper] * (cells // LANES), axis=1) if cells > LANES else upper
        cosine, sine = wave(frequency * anchor(slab, 1), period)
        real = [jnp.zeros((rows, cells), f32)] * BX
        imag = [jnp.zeros((rows, cells), f32)] * BX
        for j in range(BY):
            for i in range(BX):
                low = brick[side, i * BY + j : i * BY + j + 1, :]
                high = brick[side, (BX + i) * BY + j : (BX + i) * BY + j + 1, :]
                weight = jnp.where(top, high, low)
                real[i] = real[i] + weight * cosine
                imag[i] = imag[i] - weight * sine
            if j + 1 < BY:
                cosine, sine = (
                    cosine * wide_cos - sine * wide_sin,
                    cosine * wide_sin + sine * wide_cos,
                )
        masks = slab_masks(slab)
        placed = []
        for x in range(thick):
            parts = []
            for source in (real, imag):
                total = None
                for i in range(BX):
                    if 0 <= x - i < starts:
                        piece = source[i] * masks[x - i]
                        total = piece if total is None else total + piece
                parts.append(total)
            placed.append(jnp.concatenate(parts, axis=1))
        operand = split(jnp.concatenate(placed, axis=0))
        yield
        return product(operand, (turns_high[slab], turns_low[slab]), NT)

    def put(x, value):
        for part, ref in enumerate(planes):
            ref[pl.ds(x, rows, stride=pitch), :] = value[:, part * wide : (part + 1) * wide]

    def get(x):
        return jnp.concatenate([ref[pl.ds(x, rows, stride=pitch), :] for ref in planes], axis=1)

    def swapped(value):
        return jnp.concatenate([value[:, wide:], -value[:, :wide]], axis=1)

    pairs = pairs_of(slabs, per_slab)

    @pl.loop(0, slabs // 2 // pairs)
    def _(step):
        first = [step * pairs + n for n in range(pairs)]
        both = [slab for m in first for slab in (m, slabs - 1 - m)]
        found = side_by_side([deposit(slab, side) for side, slab in enumerate(both)])
        last = carry[...]
        for n, m in enumerate(first):
            near, far = found[2 * n], found[2 * n + 1]
            for r in range(thick):
                x = m * thick + r
                one = near[r * rows : (r + 1) * rows]
                two = last if r == 0 else far[(thick - r) * rows : (thick - r + 1) * rows]
                put(x, one + two)
                put(half + x, swapped(one - two))
            last = far[:rows]
        carry[...] = last

    put(half, carry[...])
    green_copy.wait()

    def padded(kernel):
        gap = wide - kernel.shape[1]
        if gap == 0:
            return kernel
        return jnp.concatenate([kernel, jnp.zeros((kernel.shape[0], gap), f32)], axis=1)

    def transformed(table_ref, value):
        high, low = split(value)
        return lax.dot_general(
            table_ref[...], jnp.concatenate([high, low, high], axis=0), NN, preferred_element_type=f32
        )

    together = 2 if second % 2 == 0 else 1

    @pl.loop(0, second // together)
    def _(step):
        frequencies = [step * together + n for n in range(together)]
        places = [
            pl.ds(pl.multiple_of((c * second + v) * pitch, 8), grid)
            for v in frequencies
            for c in range(2)
        ]
        inside = jnp.concatenate([ref[place, :] for place in places for ref in planes], axis=1)
        spectrum = transformed(forward_ref, inside)
        outside = []
        for n, v in enumerate(frequencies):
            for c in range(2):
                zero, one = padded(green_ref[v, c, 0]), padded(green_ref[v, c, 1])
                for part in range(2):
                    at = (4 * n + part) * wide
                    outside.append(
                        zero * spectrum[:, at : at + wide]
                        + one * spectrum[:, at + 2 * wide : at + 3 * wide]
                    )
        result = transformed(back_ref, jnp.concatenate(outside, axis=1))
        for n, place in enumerate(places):
            for part, ref in enumerate(planes):
                at = (2 * n + part) * wide
                ref[place, :] = result[:, at : at + wide]

    def evaluate(slab, inputs, side):
        masks = slab_masks(slab)
        both, spread = spread_of(slab)
        operand = split(jnp.concatenate(inputs, axis=0))
        yield
        found = product(operand, (turns_high[slab], turns_low[slab]))
        yield
        twice = [jnp.concatenate([mask, mask], axis=1) for mask in masks]
        for i in range(BX):
            total = None
            for s in range(starts):
                piece = found[(s + i) * rows : (s + i + 1) * rows] * twice[s]
                total = piece if total is None else total + piece
            chosen[side, i * rows : (i + 1) * rows, :] = total
        cell = anchor(slab, 1) + rows_iota((BY, cells)).astype(f32)
        cosine, sine = wave(cell * first_v, period)
        turn_cos, turn_sin = wave(cell, period)
        sums = [jnp.zeros((BY, cells), f32)] * (2 * BX)
        for v in range(second):
            for c in range(2):
                for i in range(BX):
                    at = i * rows + c * second + v
                    sums[c * BX + i] = (
                        sums[c * BX + i]
                        + chosen[side, at : at + 1, :cells] * cosine
                        - chosen[side, at : at + 1, cells:] * sine
                    )
            if v + 1 < second:
                cosine, sine = cosine * turn_cos - sine * turn_sin, cosine * turn_sin + sine * turn_cos
        summed = jnp.concatenate(sums, axis=0)
        masked = [jnp.where(piece_of == t, summed, 0.0) for t in range(chunks)]
        operand = split(jnp.concatenate(masked, axis=0))
        yield
        at_atoms = product(operand, spread)
        yield
        for t in range(chunks):
            _, (along_x, along_y, _) = both[t]
            pair = []
            for c in range(2):
                total = None
                for i in range(BX):
                    at = (t * 2 * BX + c * BX + i) * BY
                    piece = at_atoms[at : at + BY] * along_x[i]
                    total = piece if total is None else total + piece
                pair.append(jnp.sum(total * along_y, axis=0, keepdims=True))
            one = jnp.where(left_half, pair[0], pltpu.roll(pair[1], LANES // 2, 1))
            two = jnp.where(left_half, pltpu.roll(pair[0], LANES // 2, 1), pair[1])
            potential[pl.ds(slab * per_slab * NB + 2 * t, 1), :] = one
            potential[pl.ds(slab * per_slab * NB + 2 * t + 1, 1), :] = two

    def straight(x):
        even = get(x)
        odd = get(jnp.minimum(half + x, grid - 1)) * jnp.where((x > 0) & (x < half), 1.0, 0.0)
        turned = jnp.concatenate([-odd[:, wide:], odd[:, :wide]], axis=1)
        return even + turned, even - turned

    @pl.loop(0, slabs // 2 // pairs)
    def _(step):
        works = []
        for n in range(pairs):
            m = step * pairs + n
            near, far = [], [None] * thick
            for r in range(thick):
                ahead, behind = straight(m * thick + r)
                near.append(ahead)
                if r > 0:
                    far[thick - r] = behind
            far[0] = straight(m * thick + thick)[1]
            works.append(evaluate(m, near, 2 * n))
            works.append(evaluate(slabs - 1 - m, far, 2 * n + 1))
        side_by_side(works)

    @pl.loop(0, domains)
    def _(domain):
        out_ref[domain, NB + 2 * NH :, :] = jnp.zeros((16 - NB - 2 * NH, LANES), f32)
        out_ref[domain, :NB, :] = potential[pl.ds(pl.multiple_of(domain * NB, NB), NB), :]
        below = lax.rem(domain + domains - 1, domains)
        above = lax.rem(domain + 1, domains)
        for s in range(NH):
            at = below * NB + exports_ref[below, s]
            out_ref[domain, NB + s : NB + s + 1, :] = potential[pl.ds(at, 1), :]
            at = above * NB + exports_ref[above, NH + s]
            out_ref[domain, NB + NH + s : NB + NH + s + 1, :] = potential[pl.ds(at, 1), :]


def pairs_of(slabs, per_slab):
    if per_slab <= 2 and slabs % 8 == 0:
        return 4
    return 2 if slabs % 4 == 0 else 1


def build_reciprocal(grid, slabs, per_slab, second, depth, depth_rows):
    domains = slabs * per_slab
    cells = per_slab * NB * BZ
    sides = 2 * pairs_of(slabs, per_slab)
    return pl.pallas_call(
        functools.partial(reciprocal_kernel, grid, slabs, per_slab, second, depth),
        in_specs=[SMEM, SMEM, VMEM, pl.BlockSpec(memory_space=pl.ANY), VMEM, VMEM],
        out_specs=VMEM,
        out_shape=jax.ShapeDtypeStruct((domains, 16, LANES), f32),
        scratch_shapes=[
            pltpu.VMEM((second, 2, 2, grid, depth_rows), f32),
            pltpu.SemaphoreType.DMA,
            pltpu.VMEM((2 * second * (grid + 8), depth), f32),
            pltpu.VMEM((2 * second * (grid + 8), depth), f32),
            pltpu.VMEM((slabs, 2 * depth, 2 * cells), bf16),
            pltpu.VMEM((slabs, 2 * depth, 2 * cells), bf16),
            pltpu.VMEM((sides, 2 * BX * BY, cells), f32),
            pltpu.VMEM((2 * second, 2 * depth), f32),
            pltpu.VMEM((2 * second, LANES), f32),
            pltpu.VMEM((2 * second, LANES), f32),
            pltpu.VMEM((sides, depth, cells), f32),
            pltpu.VMEM((sides, depth, cells), f32),
            pltpu.VMEM((sides, BX * 2 * second, 2 * cells), f32),
            pltpu.VMEM((domains * NB, LANES), f32),
        ],
        compiler_params=params(),
    )


VMEM = pl.BlockSpec(memory_space=pltpu.VMEM)
SMEM = pl.BlockSpec(memory_space=pltpu.SMEM)


def per_device(
    features,
    positions,
    value_one,
    output_one,
    radial_one,
    value_two,
    output_two,
    radial_two,
    charge_weight,
    return_weight,
    green_kernel,
    exports,
    export_counts,
    brick_anchor,
):
    axes = ("dom", "rec")
    slabs, per_slab = lax.axis_size("dom"), lax.axis_size("rec")
    domains = slabs * per_slab
    atoms, width = features.shape
    depth_rows, grid, second = green_kernel.shape[0], green_kernel.shape[3], green_kernel.shape[4]
    depth = -(-depth_rows // LANES) * LANES
    chunks = atoms // LANES
    payload_rows = 5 * chunks + 4
    base = NH * BA

    def shape(*dims):
        return jax.ShapeDtypeStruct(dims, f32)

    def around(rows, by):
        return lax.ppermute(rows, axes, [(i, (i + by) % domains) for i in range(domains)])

    up, down, payload = pl.pallas_call(
        head_kernel,
        in_specs=[VMEM] * 4 + [SMEM] * 2,
        out_specs=[VMEM] * 3,
        out_shape=[
            shape(base + 8, width), shape(base + 8, width), shape(domains, payload_rows, LANES)
        ],
        scratch_shapes=[pltpu.VMEM((payload_rows, LANES), f32)],
        compiler_params=params(),
    )(features, positions, charge_weight.T, brick_anchor, exports, export_counts)

    up, down, features, green_kernel = lax.optimization_barrier((up, down, features, green_kernel))
    up = around(up, 1)
    down = around(down, -1)
    own = pl.pallas_call(
        first_own_kernel,
        in_specs=[VMEM] * 4,
        out_specs=VMEM,
        out_shape=shape(atoms, width),
        scratch_shapes=[pltpu.VMEM((atoms, width), f32)],
        compiler_params=params(),
    )(features, positions, value_one, radial_one)
    green = jnp.transpose(green_kernel, (4, 1, 2, 3, 0))
    payload, own, green, up, down = lax.optimization_barrier((payload, own, green, up, down))
    everyone = lax.all_to_all(payload, axes, 0, 0, tiled=True)

    hidden, values_two, up_two, down_two, ghost_places = pl.pallas_call(
        first_layer_kernel,
        in_specs=[VMEM] * 9 + [SMEM],
        out_specs=[VMEM] * 5,
        out_shape=[
            shape(atoms, width), shape(atoms, width), shape(base, width), shape(base, width),
            shape(8, width),
        ],
        scratch_shapes=[
            pltpu.VMEM((2 * base, width), f32),
            pltpu.VMEM((atoms, width), f32),
        ],
        compiler_params=params(),
    )(features, own, up, down, positions, value_one, output_one, radial_one, value_two, exports)

    everyone, hidden = lax.optimization_barrier((everyone, hidden))
    up_two = around(up_two, 1)
    down_two = around(down_two, -1)

    place = jnp.stack(
        [lax.axis_index("dom"), lax.axis_index("rec"), jnp.int32(depth_rows)]
    ).astype(jnp.int32)
    all_exports = everyone[:, 5 * chunks + 3, :8].astype(jnp.int32)
    table, table_back = transform_tables(grid)
    outgoing = build_reciprocal(grid, slabs, per_slab, second, depth, depth_rows)(
        place, all_exports, everyone, green, table, table_back
    )

    outgoing, up_two, down_two = lax.optimization_barrier((outgoing, up_two, down_two))
    received = lax.all_to_all(outgoing, axes, 0, 0, tiled=True)

    messages, returned = pl.pallas_call(
        second_layer_kernel,
        in_specs=[VMEM] * 8,
        out_specs=[VMEM] * 2,
        out_shape=[shape(atoms, width), shape(8, width)],
        scratch_shapes=[pltpu.VMEM((2 * base, width), f32)],
        compiler_params=params(),
    )(values_two, up_two, down_two, ghost_places, positions, radial_two, return_weight, value_two)

    return pl.pallas_call(
        tail_kernel,
        in_specs=[VMEM] * 9,
        out_specs=VMEM,
        out_shape=shape(atoms, width),
        compiler_params=params(),
    )(
        received, messages, hidden, ghost_places, positions, radial_two, return_weight, returned, output_two
    )


def solution(mesh):
    placed = (
        P(("dom", "rec"), None),
        P(None, ("dom", "rec")),
        P(),
        P(),
        P(),
        P(),
        P(),
        P(),
        P(),
        P(),
        P("rec", None, None, None, "dom"),
        P(("dom", "rec"), None, None),
        P(("dom", "rec"), None),
        P(None, ("dom", "rec")),
    )
    return jax.shard_map(
        per_device, mesh=mesh, in_specs=placed, out_specs=P(("dom", "rec"), None), check_vma=False
    )
```

```python
import functools
import math

import jax
import jax.numpy as jnp
import numpy as np
from jax import lax
from jax.experimental import pallas as pl
from jax.experimental.pallas import tpu as pltpu
from jax.sharding import PartitionSpec as P

BA = 64
BX = 4
BY = 8
BZ = 8
NB = 8
NH = 3
NR = 8
LANES = 128

soften = 0.01
norm_epsilon = 1e-05
f32 = jnp.float32
bf16 = jnp.bfloat16
NN = (((1,), (0,)), ((), ()))
NT = (((1,), (1,)), ((), ()))
STEP = 12.0 / 7.0
OWN_GROUP = 4
FACTORS = np.exp(-18.0 * np.arange(NR) ** 2 / 49.0).astype(np.float32)


def params(mib=60):
    return pltpu.CompilerParams(vmem_limit_bytes=mib * 1024 * 1024)


def split(value):
    high = value.astype(bf16)
    return high, (value - high.astype(f32)).astype(bf16)


def product(left, right, dims=NN):
    axis = dims[0][1][0]
    return lax.dot_general(
        jnp.concatenate([left[0], left[0], left[1]], axis=1),
        jnp.concatenate([right[0], right[1], right[0]], axis=axis),
        dims,
        preferred_element_type=f32,
    )


def narrow_product(left, right):
    def one(a, b):
        return lax.dot_general(a, b, NN, preferred_element_type=f32)

    return one(left[0], right[0]) + (one(left[0], right[1]) + one(left[1], right[0]))


def wave(phase, period):
    rest = phase - period * jnp.floor(phase * (1.0 / period) + 0.5)
    turn = rest * (1.0 / period)
    square = turn * turn
    cosine = jnp.full_like(turn, (-1) ** 9 * (2 * math.pi) ** 18 / math.factorial(18))
    sine = jnp.full_like(turn, (-1) ** 9 * (2 * math.pi) ** 19 / math.factorial(19))
    for n in range(8, -1, -1):
        cosine = cosine * square + (-1) ** n * (2 * math.pi) ** (2 * n) / math.factorial(2 * n)
        sine = sine * square + (-1) ** n * (2 * math.pi) ** (2 * n + 1) / math.factorial(2 * n + 1)
    return cosine, sine * turn


def rows_iota(shape):
    return lax.broadcasted_iota(jnp.int32, shape, len(shape) - 2)


def lanes_iota(shape):
    return lax.broadcasted_iota(jnp.int32, shape, len(shape) - 1)


def side_by_side(works):
    results = [None] * len(works)
    waiting = list(range(len(works)))
    while waiting:
        for n in list(waiting):
            try:
                next(works[n])
            except StopIteration as end:
                results[n] = end.value
                waiting.remove(n)
    return results


def pack_places(out_ref, places_ref, exports_ref, counts_ref, side):
    base = NH * BA
    out_ref[base : base + 8, :] = jnp.zeros((8, out_ref.shape[1]), f32)
    for s in range(NH):
        chosen = exports_ref[0, side, s]
        lane = side * base + s * BA
        found = places_ref[:, :BA]
        for b in range(1, NB):
            found = jnp.where(chosen == b, places_ref[:, b * BA : (b + 1) * BA], found)
        out_ref[base : base + 3, lane : lane + BA] = found
        live = jnp.where(s < counts_ref[0, side], 1.0, 0.0)
        out_ref[base + 3 : base + 4, lane : lane + BA] = jnp.full((1, BA), live, f32)


def pack_rows(out_ref, rows_ref, exports_ref, side):
    for s in range(NH):
        start = pl.multiple_of(exports_ref[0, side, s] * BA, BA)
        out_ref[s * BA : (s + 1) * BA, :] = rows_ref[pl.ds(start, BA), :]


def head_kernel(
    features_ref, places_ref, charge_ref, anchor_ref, exports_ref, counts_ref,
    up_ref, down_ref, payload_ref,
    staged,
):
    for out_ref, side in ((up_ref, 0), (down_ref, 1)):
        pack_rows(out_ref, features_ref, exports_ref, side)
        pack_places(out_ref, places_ref, exports_ref, counts_ref, side)
    charge_rows = jnp.concatenate(
        [charge_ref[...], jnp.zeros((6, charge_ref.shape[1]), f32)], axis=0
    )
    charges = product(split(charge_rows), split(features_ref[...]), NT)
    chunks = features_ref.shape[0] // LANES
    for t in range(chunks):
        lane = slice(t * LANES, (t + 1) * LANES)
        for c in range(2):
            staged[c * chunks + t : c * chunks + t + 1, :] = charges[c : c + 1, lane]
        for d in range(3):
            row = (2 + d) * chunks + t
            staged[row : row + 1, :] = places_ref[d : d + 1, lane]
    anchors = anchor_ref[...].astype(f32)
    block = lanes_iota((3, LANES)) % (NB * BZ) // BZ
    spread = jnp.broadcast_to(anchors[:, :1], (3, LANES))
    for b in range(1, NB):
        spread = jnp.where(block == b, anchors[:, b : b + 1], spread)
    staged[5 * chunks : 5 * chunks + 3, :] = spread
    lane = lanes_iota((1, LANES))
    listed = jnp.zeros((1, LANES), jnp.int32)
    for side in range(2):
        for s in range(NH):
            listed = jnp.where(lane == side * NH + s, exports_ref[0, side, s], listed)
    staged[5 * chunks + 3 :, :] = listed.astype(f32)
    payload = staged[...]

    @pl.loop(0, payload_ref.shape[0])
    def _(domain):
        payload_ref[domain] = payload


def pair_terms(squared, live):
    softened = squared + soften
    near = jnp.exp(-2.0 * softened)
    if live is not None:
        near = near * live
    return near, jnp.exp(STEP * (softened * lax.rsqrt(softened)))


def squared_distance(columns, rows):
    total = None
    for d in range(3):
        delta = columns[:, d : d + 1] - rows[d : d + 1, :]
        total = delta * delta if total is None else total + delta * delta
    return total


def scaled_weights(weight_ref):
    return [weight_ref[k : k + 1, :] * float(FACTORS[k]) for k in range(NR)]


def place_columns(places_ref):
    atoms = places_ref.shape[1]
    return jnp.transpose(jnp.concatenate([places_ref[...], jnp.zeros((5, atoms), f32)], axis=0))


def ghost_messages(ghost_values_ref, places_ref, ghost_places, weight_ref):
    weights = scaled_weights(weight_ref)
    ghosts = 2 * NH * BA
    near, ratio = pair_terms(
        squared_distance(place_columns(places_ref), ghost_places[:, :ghosts]),
        ghost_places[3:4, :ghosts],
    )
    term = near

    def operands(k):
        nonlocal term
        after = term * ratio
        left = split(jnp.concatenate([term, after], axis=1))
        term = after * ratio
        values = ghost_values_ref[...]
        return left, split(
            jnp.concatenate([values * weights[k], values * weights[k + 1]], axis=0)
        )

    total = None
    ready = operands(0)
    for k in range(0, NR, 2):
        following = operands(k + 2) if k + 2 < NR else None
        part = product(*ready)
        total = part if total is None else total + part
        ready = following
    return total


def own_messages(values_ref, places_ref, weight_ref, out_ref):
    weights = scaled_weights(weight_ref)
    atoms = values_ref.shape[0]
    columns = place_columns(places_ref)
    half = lanes_iota((BA, 2 * BA)) >= BA
    partner = lanes_iota((BA, 2 * BA)) % BA
    other = (partner != rows_iota((BA, 2 * BA))).astype(f32)

    def one_block(b):
        rows = slice(b * BA, (b + 1) * BA)
        here = places_ref[:, rows]
        near, ratio = pair_terms(
            squared_distance(columns[rows], jnp.concatenate([here, here], axis=1)), other
        )
        term = jnp.where(half, near * ratio, near)
        ratio = ratio * ratio
        lefts, rights = [], []
        values = values_ref[rows, :]
        for k in range(0, NR, 2):
            lefts.append(term)
            rights.append(values * weights[k])
            rights.append(values * weights[k + 1])
            term = term * ratio
        left = split(jnp.concatenate(lefts, axis=1))
        right = split(jnp.concatenate(rights, axis=0))
        yield
        out_ref[rows, :] = product(left, right)

    blocks = atoms // BA
    for b in range(0, blocks, OWN_GROUP):
        side_by_side([one_block(b + n) for n in range(OWN_GROUP)])


def finish(hidden, messages, output_ref):
    scaled = messages * lax.rsqrt(
        jnp.mean(messages * messages, axis=-1, keepdims=True) + norm_epsilon
    )
    active = scaled / (1.0 + jnp.exp(-scaled))
    return hidden + product(split(active), split(output_ref[...]))


def first_own_kernel(
    features_ref, places_ref, value_one_ref, weight_ref, return_ref, value_two_ref,
    messages_ref, returned_ref,
    values,
):
    values[...] = product(split(features_ref[...]), split(value_one_ref[...]))
    own_messages(values, places_ref, weight_ref, messages_ref)
    return_rows = jnp.concatenate(
        [return_ref[...], jnp.zeros((6, return_ref.shape[1]), f32)], axis=0
    )
    returned_ref[...] = product(split(return_rows), split(value_two_ref[...]))


def fetched(sources, targets, arrived):
    copies = [
        pltpu.make_async_copy(source, target, arrived.at[n])
        for n, (source, target) in enumerate(zip(sources, targets))
    ]
    for copy in copies:
        copy.start()
    return copies


def first_layer_kernel(
    up_ref, down_ref, places_ref, value_one_ref, weight_ref, exports_ref,
    features_hbm, own_hbm, output_one_hbm, value_two_hbm,
    hidden_ref, values_two_ref, up_two_ref, down_two_ref, ghost_places_ref,
    ghost_values, features_ref, own_ref, output_one_ref, value_two_ref, arrived,
):
    copies = fetched(
        (features_hbm, own_hbm, output_one_hbm, value_two_hbm),
        (features_ref, own_ref, output_one_ref, value_two_ref),
        arrived,
    )
    base = NH * BA
    ghost_rows = jnp.concatenate([up_ref[:base, :], down_ref[:base, :]], axis=0)
    ghost_values[...] = product(split(ghost_rows), split(value_one_ref[...]))
    ghost_places_ref[...] = up_ref[base : base + 8, :] + down_ref[base : base + 8, :]
    messages = ghost_messages(ghost_values, places_ref, ghost_places_ref[...], weight_ref)
    for copy in copies:
        copy.wait()
    hidden_ref[...] = finish(features_ref[...], own_ref[...] + messages, output_one_ref)
    values_two_ref[...] = product(split(hidden_ref[...]), split(value_two_ref[...]))
    pack_rows(up_two_ref, values_two_ref, exports_ref, 0)
    pack_rows(down_two_ref, values_two_ref, exports_ref, 1)


def second_layer_kernel(
    values_ref, up_two_ref, down_two_ref, ghost_places_ref, places_ref, weight_ref,
    messages_ref,
    ghost_values,
):
    base = NH * BA
    ghost_values[:base, :] = up_two_ref[...]
    ghost_values[base:, :] = down_two_ref[...]
    own_messages(values_ref, places_ref, weight_ref, messages_ref)
    messages_ref[...] += ghost_messages(
        ghost_values, places_ref, ghost_places_ref[...], weight_ref
    )


def tail_kernel(
    received_ref, ghost_places_ref, places_ref, weight_ref, return_ref, returned_ref,
    messages_hbm, hidden_hbm, output_two_hbm,
    updated_ref,
    messages_ref, hidden_ref, output_two_ref, arrived,
):
    copies = fetched(
        (messages_hbm, hidden_hbm, output_two_hbm),
        (messages_ref, hidden_ref, output_two_ref),
        arrived,
    )
    atoms = hidden_ref.shape[0]
    ghosts = 2 * NH * BA
    potentials = jnp.sum(received_ref[...], axis=0)
    columns = jnp.transpose(potentials)
    ghost_places = ghost_places_ref[...]
    ghost_columns = jnp.transpose(ghost_places[:, :ghosts])
    own_columns = jnp.transpose(
        jnp.concatenate([places_ref[...], jnp.zeros((5, atoms), f32)], axis=0)
    )
    half = lanes_iota((BA, LANES)) >= BA
    other = (lanes_iota((BA, LANES)) % BA != rows_iota((BA, LANES))).astype(f32)
    ghost_potential = [
        jnp.concatenate([columns[c * BA : (c + 1) * BA, NB + s : NB + s + 1] for s in range(2 * NH)], axis=0)
        for c in range(2)
    ]
    pieces = []
    for t in range(atoms // LANES):
        lane = slice(t * LANES, (t + 1) * LANES)
        here = places_ref[:, lane]
        near, ratio = pair_terms(squared_distance(ghost_columns, here), ghost_columns[:, 3:4])
        squared = None
        own_potential = []
        for c in range(2):
            own_potential.append(
                jnp.where(
                    half,
                    columns[c * BA : (c + 1) * BA, 2 * t + 1 : 2 * t + 2],
                    columns[c * BA : (c + 1) * BA, 2 * t : 2 * t + 1],
                )
            )
        for d in range(3):
            first = own_columns[2 * t * BA : (2 * t + 1) * BA, d : d + 1]
            second = own_columns[(2 * t + 1) * BA : (2 * t + 2) * BA, d : d + 1]
            delta = jnp.where(half, second, first) - here[d : d + 1, :]
            squared = delta * delta if squared is None else squared + delta * delta
        own_near, own_ratio = pair_terms(squared, other)
        ratio = jnp.concatenate([ratio, own_ratio], axis=0)
        terms = [
            jnp.concatenate([near * ghost_potential[c], own_near * own_potential[c]], axis=0)
            for c in range(2)
        ]
        sums = [None] * (2 * NR)
        for start in range(0, ratio.shape[0], 8):
            tile = slice(start, start + 8)
            step = ratio[tile]
            for c in range(2):
                term = terms[c][tile]
                for k in range(NR):
                    at = 2 * k + c
                    sums[at] = term if sums[at] is None else sums[at] + term
                    if k + 1 < NR:
                        term = term * step
        pieces.append(
            jnp.concatenate([jnp.sum(total, axis=0, keepdims=True) for total in sums], axis=0)
        )
    gathered = jnp.transpose(jnp.concatenate(pieces, axis=1))
    spread = jnp.concatenate(
        [
            returned_ref[c : c + 1, :] * (weight_ref[k : k + 1, :] * float(FACTORS[k]))
            for k in range(NR)
            for c in range(2)
        ],
        axis=0,
    )
    for copy in copies:
        copy.wait()
    messages = messages_ref[...] + narrow_product(split(gathered), split(spread))
    back = [return_ref[c : c + 1, :] for c in range(2)]
    layer_input = jnp.concatenate(
        [
            hidden_ref[b * BA : (b + 1) * BA, :]
            + columns[:BA, b : b + 1] * back[0]
            + columns[BA:, b : b + 1] * back[1]
            for b in range(atoms // BA)
        ],
        axis=0,
    )
    updated_ref[...] = finish(layer_input, messages, output_two_ref)


def transform_tables(grid):
    half = grid // 2
    u = np.arange(grid)
    x = np.concatenate([np.arange(half + 1), np.arange(1, half)])
    angle = 2.0 * np.pi * (np.outer(u, x) % grid) / grid
    table = np.where(np.arange(grid)[None] <= half, np.cos(angle), np.sin(angle)).astype(np.float32)
    back = (table.T / float(grid) ** 3).astype(np.float32)

    def halves(value):
        high = value.astype(bf16)
        low = (value - high.astype(np.float32)).astype(bf16)
        return np.concatenate([high, high, low], axis=1)

    return halves(table), halves(back)


def reciprocal_kernel(
    grid, slabs, per_slab, second, depth,
    exports_ref, payload_ref, green_hbm, forward_ref, back_ref,
    out_ref,
    green_ref, green_arrived, planes_real, planes_imag, turns_high, turns_low, brick, carry,
    shift_cos, shift_sin, stage_cos, stage_sin, chosen, potential,
):
    green_copy = pltpu.make_async_copy(green_hbm, green_ref, green_arrived)
    green_copy.start()
    planes = (planes_real, planes_imag)
    domains = slabs * per_slab
    half = grid // 2
    pitch = grid + 8
    thick = grid // slabs
    starts = thick - BX + 1
    rows = 2 * second
    cells = per_slab * NB * BZ
    atoms = per_slab * NB * BA
    chunks = atoms // LANES
    own = NB * BA // LANES
    wide = depth
    first_v = (lax.axis_index("dom") * second).astype(f32)
    first_w = (lax.axis_index("rec") * green_hbm.shape[4]).astype(f32)
    period = float(grid)

    row = rows_iota((rows, 1))
    frequency = jnp.where(row >= second, row - second, row).astype(f32) + first_v
    cosine, sine = wave(jnp.broadcast_to(frequency, (rows, LANES)), period)
    shift_cos[...] = cosine
    shift_sin[...] = sine
    upper = rows_iota((rows, LANES)) >= second
    carry[...] = jnp.zeros(carry.shape, f32)
    left_half = lanes_iota((1, LANES)) < LANES // 2

    def atom_rows(slab, t):
        base = slab * per_slab + t // own
        return [payload_ref[base, q * own + t % own : q * own + t % own + 1, :] for q in range(5)]

    def windows(parts):
        cell = rows_iota((BY, LANES)).astype(f32)
        along_x = [jnp.exp(-((float(i) - parts[2] * 1.5) ** 2)) for i in range(BX)]
        along_y = jnp.exp(-((cell - parts[3] * 3.5) ** 2))
        along_z = jnp.exp(-((cell - parts[4] * 3.5) ** 2))
        return along_x, along_y, along_z

    def anchor(slab, dim):
        found = []
        for q in range(0, per_slab, 2):
            one = payload_ref[slab * per_slab + q, 5 * own + dim : 5 * own + dim + 1, :]
            two = payload_ref[slab * per_slab + q + 1, 5 * own + dim : 5 * own + dim + 1, :]
            found.append(jnp.where(left_half, one, two))
        return jnp.concatenate(found, axis=1) if len(found) > 1 else found[0]

    def spread_of(slab):
        both, pieces = [], []
        for t in range(chunks):
            parts = atom_rows(slab, t)
            along = windows(parts)
            pieces.append(jnp.where(left_half, along[2], 0.0))
            pieces.append(jnp.where(left_half, 0.0, along[2]))
            both.append((parts, along))
        return both, split(jnp.concatenate(pieces, axis=0))

    piece_of = lanes_iota((1, cells)) // (2 * BZ)

    def slab_masks(slab):
        start = anchor(slab, 0) - (slab * thick).astype(f32)
        return [(start == float(s)).astype(f32) for s in range(starts)]

    def deposit(slab, side):
        both, spread = spread_of(slab)
        lefts = []
        for parts, (along_x, along_y, _) in both:
            for c in range(2):
                for i in range(BX):
                    lefts.append((parts[c] * along_x[i]) * along_y)
        operand = split(jnp.concatenate(lefts, axis=0))
        yield
        found = product(operand, spread, NT)
        yield
        height = 2 * BX * BY
        total = found[:height]
        for t in range(1, chunks):
            total = jnp.where(piece_of == t, found[t * height : (t + 1) * height], total)
        brick[side] = total
        low_cell = anchor(slab, 2) + (lanes_iota((1, cells)) % BZ).astype(f32)
        ramp = rows_iota((8, cells)).astype(f32) + first_w
        cosine, sine = wave(ramp * low_cell, period)
        turn_cos, turn_sin = wave(8.0 * low_cell, period)
        for g in range(wide // 8):
            at = slice(g * 8, (g + 1) * 8)
            stage_cos[side, at, :] = cosine
            stage_sin[side, at, :] = sine
            cosine, sine = cosine * turn_cos - sine * turn_sin, cosine * turn_sin + sine * turn_cos
        cos_high, cos_low = split(stage_cos[side])
        sin_high, sin_low = split(stage_sin[side])
        for ref, c_part, s_part in ((turns_high, cos_high, sin_high), (turns_low, cos_low, sin_low)):
            ref[slab, :wide, :cells] = c_part
            ref[slab, :wide, cells:] = s_part
            ref[slab, wide:, :cells] = -s_part
            ref[slab, wide:, cells:] = c_part
        wide_cos = jnp.concatenate([shift_cos[...]] * (cells // LANES), axis=1)
        wide_sin = jnp.concatenate([shift_sin[...]] * (cells // LANES), axis=1)
        top = jnp.concatenate([upper] * (cells // LANES), axis=1) if cells > LANES else upper
        cosine, sine = wave(frequency * anchor(slab, 1), period)
        real = [jnp.zeros((rows, cells), f32)] * BX
        imag = [jnp.zeros((rows, cells), f32)] * BX
        for j in range(BY):
            for i in range(BX):
                low = brick[side, i * BY + j : i * BY + j + 1, :]
                high = brick[side, (BX + i) * BY + j : (BX + i) * BY + j + 1, :]
                weight = jnp.where(top, high, low)
                real[i] = real[i] + weight * cosine
                imag[i] = imag[i] - weight * sine
            if j + 1 < BY:
                cosine, sine = (
                    cosine * wide_cos - sine * wide_sin,
                    cosine * wide_sin + sine * wide_cos,
                )
        masks = slab_masks(slab)
        placed = []
        for x in range(thick):
            parts = []
            for source in (real, imag):
                total = None
                for i in range(BX):
                    if 0 <= x - i < starts:
                        piece = source[i] * masks[x - i]
                        total = piece if total is None else total + piece
                parts.append(total)
            placed.append(jnp.concatenate(parts, axis=1))
        operand = split(jnp.concatenate(placed, axis=0))
        yield
        return product(operand, (turns_high[slab], turns_low[slab]), NT)

    def put(x, value):
        for part, ref in enumerate(planes):
            ref[pl.ds(x, rows, stride=pitch), :] = value[:, part * wide : (part + 1) * wide]

    def get(x):
        return jnp.concatenate([ref[pl.ds(x, rows, stride=pitch), :] for ref in planes], axis=1)

    def swapped(value):
        return jnp.concatenate([value[:, wide:], -value[:, :wide]], axis=1)

    pairs = pairs_of(slabs, per_slab)

    @pl.loop(0, slabs // 2 // pairs)
    def _(step):
        first = [step * pairs + n for n in range(pairs)]
        both = [slab for m in first for slab in (m, slabs - 1 - m)]
        found = side_by_side([deposit(slab, side) for side, slab in enumerate(both)])
        last = carry[...]
        for n, m in enumerate(first):
            near, far = found[2 * n], found[2 * n + 1]
            for r in range(thick):
                x = m * thick + r
                one = near[r * rows : (r + 1) * rows]
                two = last if r == 0 else far[(thick - r) * rows : (thick - r + 1) * rows]
                put(x, one + two)
                put(half + x, swapped(one - two))
            last = far[:rows]
        carry[...] = last

    put(half, carry[...])
    green_copy.wait()

    def padded(kernel):
        gap = wide - kernel.shape[1]
        if gap == 0:
            return kernel
        return jnp.concatenate([kernel, jnp.zeros((kernel.shape[0], gap), f32)], axis=1)

    def transformed(table_ref, value):
        high, low = split(value)
        return lax.dot_general(
            table_ref[...], jnp.concatenate([high, low, high], axis=0), NN, preferred_element_type=f32
        )

    together = 2 if second % 2 == 0 else 1

    @pl.loop(0, second // together)
    def _(step):
        frequencies = [step * together + n for n in range(together)]
        places = [
            pl.ds(pl.multiple_of((c * second + v) * pitch, 8), grid)
            for v in frequencies
            for c in range(2)
        ]
        inside = jnp.concatenate([ref[place, :] for place in places for ref in planes], axis=1)
        spectrum = transformed(forward_ref, inside)
        outside = []
        for n, v in enumerate(frequencies):
            for c in range(2):
                zero, one = padded(green_ref[v, c, 0]), padded(green_ref[v, c, 1])
                for part in range(2):
                    at = (4 * n + part) * wide
                    outside.append(
                        zero * spectrum[:, at : at + wide]
                        + one * spectrum[:, at + 2 * wide : at + 3 * wide]
                    )
        result = transformed(back_ref, jnp.concatenate(outside, axis=1))
        for n, place in enumerate(places):
            for part, ref in enumerate(planes):
                at = (2 * n + part) * wide
                ref[place, :] = result[:, at : at + wide]

    def evaluate(slab, inputs, side):
        masks = slab_masks(slab)
        both, spread = spread_of(slab)
        operand = split(jnp.concatenate(inputs, axis=0))
        yield
        found = product(operand, (turns_high[slab], turns_low[slab]))
        yield
        twice = [jnp.concatenate([mask, mask], axis=1) for mask in masks]
        for i in range(BX):
            total = None
            for s in range(starts):
                piece = found[(s + i) * rows : (s + i + 1) * rows] * twice[s]
                total = piece if total is None else total + piece
            chosen[side, i * rows : (i + 1) * rows, :] = total
        cell = anchor(slab, 1) + rows_iota((BY, cells)).astype(f32)
        cosine, sine = wave(cell * first_v, period)
        turn_cos, turn_sin = wave(cell, period)
        sums = [jnp.zeros((BY, cells), f32)] * (2 * BX)
        for v in range(second):
            for c in range(2):
                for i in range(BX):
                    at = i * rows + c * second + v
                    sums[c * BX + i] = (
                        sums[c * BX + i]
                        + chosen[side, at : at + 1, :cells] * cosine
                        - chosen[side, at : at + 1, cells:] * sine
                    )
            if v + 1 < second:
                cosine, sine = cosine * turn_cos - sine * turn_sin, cosine * turn_sin + sine * turn_cos
        summed = jnp.concatenate(sums, axis=0)
        masked = [jnp.where(piece_of == t, summed, 0.0) for t in range(chunks)]
        operand = split(jnp.concatenate(masked, axis=0))
        yield
        at_atoms = product(operand, spread)
        yield
        for t in range(chunks):
            _, (along_x, along_y, _) = both[t]
            pair = []
            for c in range(2):
                total = None
                for i in range(BX):
                    at = (t * 2 * BX + c * BX + i) * BY
                    piece = at_atoms[at : at + BY] * along_x[i]
                    total = piece if total is None else total + piece
                pair.append(jnp.sum(total * along_y, axis=0, keepdims=True))
            one = jnp.where(left_half, pair[0], pltpu.roll(pair[1], LANES // 2, 1))
            two = jnp.where(left_half, pltpu.roll(pair[0], LANES // 2, 1), pair[1])
            potential[pl.ds(slab * per_slab * NB + 2 * t, 1), :] = one
            potential[pl.ds(slab * per_slab * NB + 2 * t + 1, 1), :] = two

    def straight(x):
        even = get(x)
        odd = get(jnp.minimum(half + x, grid - 1)) * jnp.where((x > 0) & (x < half), 1.0, 0.0)
        turned = jnp.concatenate([-odd[:, wide:], odd[:, :wide]], axis=1)
        return even + turned, even - turned

    @pl.loop(0, slabs // 2 // pairs)
    def _(step):
        works = []
        for n in range(pairs):
            m = step * pairs + n
            near, far = [], [None] * thick
            for r in range(thick):
                ahead, behind = straight(m * thick + r)
                near.append(ahead)
                if r > 0:
                    far[thick - r] = behind
            far[0] = straight(m * thick + thick)[1]
            works.append(evaluate(m, near, 2 * n))
            works.append(evaluate(slabs - 1 - m, far, 2 * n + 1))
        side_by_side(works)

    @pl.loop(0, domains)
    def _(domain):
        out_ref[domain, NB + 2 * NH :, :] = jnp.zeros((16 - NB - 2 * NH, LANES), f32)
        out_ref[domain, :NB, :] = potential[pl.ds(pl.multiple_of(domain * NB, NB), NB), :]
        below = lax.rem(domain + domains - 1, domains)
        above = lax.rem(domain + 1, domains)
        for s in range(NH):
            at = below * NB + exports_ref[below, s]
            out_ref[domain, NB + s : NB + s + 1, :] = potential[pl.ds(at, 1), :]
            at = above * NB + exports_ref[above, NH + s]
            out_ref[domain, NB + NH + s : NB + NH + s + 1, :] = potential[pl.ds(at, 1), :]


def pairs_of(slabs, per_slab):
    if per_slab <= 2 and slabs % 8 == 0:
        return 4
    return 2 if slabs % 4 == 0 else 1


def build_reciprocal(grid, slabs, per_slab, second, depth, depth_rows):
    domains = slabs * per_slab
    cells = per_slab * NB * BZ
    sides = 2 * pairs_of(slabs, per_slab)
    return pl.pallas_call(
        functools.partial(reciprocal_kernel, grid, slabs, per_slab, second, depth),
        in_specs=[SMEM, VMEM, ANY, VMEM, VMEM],
        out_specs=VMEM,
        out_shape=jax.ShapeDtypeStruct((domains, 16, LANES), f32),
        scratch_shapes=[
            pltpu.VMEM((second, 2, 2, grid, depth_rows), f32),
            pltpu.SemaphoreType.DMA,
            pltpu.VMEM((2 * second * (grid + 8), depth), f32),
            pltpu.VMEM((2 * second * (grid + 8), depth), f32),
            pltpu.VMEM((slabs, 2 * depth, 2 * cells), bf16),
            pltpu.VMEM((slabs, 2 * depth, 2 * cells), bf16),
            pltpu.VMEM((sides, 2 * BX * BY, cells), f32),
            pltpu.VMEM((2 * second, 2 * depth), f32),
            pltpu.VMEM((2 * second, LANES), f32),
            pltpu.VMEM((2 * second, LANES), f32),
            pltpu.VMEM((sides, depth, cells), f32),
            pltpu.VMEM((sides, depth, cells), f32),
            pltpu.VMEM((sides, BX * 2 * second, 2 * cells), f32),
            pltpu.VMEM((domains * NB, LANES), f32),
        ],
        compiler_params=params(),
    )


VMEM = pl.BlockSpec(memory_space=pltpu.VMEM)
SMEM = pl.BlockSpec(memory_space=pltpu.SMEM)
ANY = pl.BlockSpec(memory_space=pl.ANY)


def per_device(
    features,
    positions,
    value_one,
    output_one,
    radial_one,
    value_two,
    output_two,
    radial_two,
    charge_weight,
    return_weight,
    green_kernel,
    exports,
    export_counts,
    brick_anchor,
):
    axes = ("dom", "rec")
    slabs, per_slab = lax.axis_size("dom"), lax.axis_size("rec")
    domains = slabs * per_slab
    atoms, width = features.shape
    depth_rows, grid, second = green_kernel.shape[0], green_kernel.shape[3], green_kernel.shape[4]
    depth = -(-depth_rows // LANES) * LANES
    chunks = atoms // LANES
    payload_rows = 5 * chunks + 4
    base = NH * BA

    def shape(*dims):
        return jax.ShapeDtypeStruct(dims, f32)

    def around(rows, by):
        return lax.ppermute(rows, axes, [(i, (i + by) % domains) for i in range(domains)])

    up, down, payload = pl.pallas_call(
        head_kernel,
        in_specs=[VMEM] * 4 + [SMEM] * 2,
        out_specs=[VMEM] * 3,
        out_shape=[
            shape(base + 8, width), shape(base + 8, width), shape(domains, payload_rows, LANES)
        ],
        scratch_shapes=[pltpu.VMEM((payload_rows, LANES), f32)],
        compiler_params=params(),
    )(features, positions, charge_weight.T, brick_anchor, exports, export_counts)

    up, down, features, green_kernel = lax.optimization_barrier((up, down, features, green_kernel))
    up = around(up, 1)
    down = around(down, -1)
    own, returned = pl.pallas_call(
        first_own_kernel,
        in_specs=[VMEM] * 6,
        out_specs=[VMEM] * 2,
        out_shape=[shape(atoms, width), shape(8, width)],
        scratch_shapes=[pltpu.VMEM((atoms, width), f32)],
        compiler_params=params(),
    )(features, positions, value_one, radial_one, return_weight, value_two)
    green = jnp.transpose(green_kernel, (4, 1, 2, 3, 0))
    payload, own, green, up, down = lax.optimization_barrier((payload, own, green, up, down))
    everyone = lax.all_to_all(payload, axes, 0, 0, tiled=True)

    hidden, values_two, up_two, down_two, ghost_places = pl.pallas_call(
        first_layer_kernel,
        in_specs=[VMEM] * 5 + [SMEM] + [ANY] * 4,
        out_specs=[VMEM] * 5,
        out_shape=[
            shape(atoms, width), shape(atoms, width), shape(base, width), shape(base, width),
            shape(8, width),
        ],
        scratch_shapes=[
            pltpu.VMEM((2 * base, width), f32),
            pltpu.VMEM((atoms, width), f32),
            pltpu.VMEM((atoms, width), f32),
            pltpu.VMEM((width, width), f32),
            pltpu.VMEM((width, width), f32),
            pltpu.SemaphoreType.DMA((4,)),
        ],
        compiler_params=params(),
    )(up, down, positions, value_one, radial_one, exports, features, own, output_one, value_two)

    everyone, hidden = lax.optimization_barrier((everyone, hidden))
    up_two = around(up_two, 1)
    down_two = around(down_two, -1)

    all_exports = everyone[:, 5 * chunks + 3, :8].astype(jnp.int32)
    table, table_back = transform_tables(grid)
    outgoing = build_reciprocal(grid, slabs, per_slab, second, depth, depth_rows)(
        all_exports, everyone, green, table, table_back
    )

    outgoing, up_two, down_two = lax.optimization_barrier((outgoing, up_two, down_two))
    received = lax.all_to_all(outgoing, axes, 0, 0, tiled=True)

    messages = pl.pallas_call(
        second_layer_kernel,
        in_specs=[VMEM] * 6,
        out_specs=VMEM,
        out_shape=shape(atoms, width),
        scratch_shapes=[pltpu.VMEM((2 * base, width), f32)],
        compiler_params=params(),
    )(values_two, up_two, down_two, ghost_places, positions, radial_two)

    return pl.pallas_call(
        tail_kernel,
        in_specs=[VMEM] * 6 + [ANY] * 3,
        out_specs=VMEM,
        out_shape=shape(atoms, width),
        scratch_shapes=[
            pltpu.VMEM((atoms, width), f32),
            pltpu.VMEM((atoms, width), f32),
            pltpu.VMEM((width, width), f32),
            pltpu.SemaphoreType.DMA((3,)),
        ],
        compiler_params=params(),
    )(
        received, ghost_places, positions, radial_two, return_weight, returned,
        messages, hidden, output_two,
    )


def solution(mesh):
    placed = (
        P(("dom", "rec"), None),
        P(None, ("dom", "rec")),
        P(),
        P(),
        P(),
        P(),
        P(),
        P(),
        P(),
        P(),
        P("rec", None, None, None, "dom"),
        P(("dom", "rec"), None, None),
        P(("dom", "rec"), None),
        P(None, ("dom", "rec")),
    )
    return jax.shard_map(
        per_device, mesh=mesh, in_specs=placed, out_specs=P(("dom", "rec"), None), check_vma=False
    )
```

```python
import functools
import math

import jax
import jax.numpy as jnp
import numpy as np
from jax import lax
from jax.experimental import pallas as pl
from jax.experimental.pallas import tpu as pltpu
from jax.sharding import PartitionSpec as P

BA = 64
BX = 4
BY = 8
BZ = 8
NB = 8
NH = 3
NR = 8
LANES = 128

soften = 0.01
norm_epsilon = 1e-05
f32 = jnp.float32
bf16 = jnp.bfloat16
NN = (((1,), (0,)), ((), ()))
NT = (((1,), (1,)), ((), ()))
STEP = 12.0 / 7.0
OWN_GROUP = 4
FACTORS = np.exp(-18.0 * np.arange(NR) ** 2 / 49.0).astype(np.float32)


def params(mib=60):
    return pltpu.CompilerParams(vmem_limit_bytes=mib * 1024 * 1024)


def split(value):
    high = value.astype(bf16)
    return high, (value - high.astype(f32)).astype(bf16)


def product(left, right, dims=NN):
    axis = dims[0][1][0]
    return lax.dot_general(
        jnp.concatenate([left[0], left[0], left[1]], axis=1),
        jnp.concatenate([right[0], right[1], right[0]], axis=axis),
        dims,
        preferred_element_type=f32,
    )


def narrow_product(left, right):
    def one(a, b):
        return lax.dot_general(a, b, NN, preferred_element_type=f32)

    return one(left[0], right[0]) + (one(left[0], right[1]) + one(left[1], right[0]))


def wave(phase, period):
    rest = phase - period * jnp.floor(phase * (1.0 / period) + 0.5)
    turn = rest * (1.0 / period)
    square = turn * turn
    cosine = jnp.full_like(turn, (-1) ** 9 * (2 * math.pi) ** 18 / math.factorial(18))
    sine = jnp.full_like(turn, (-1) ** 9 * (2 * math.pi) ** 19 / math.factorial(19))
    for n in range(8, -1, -1):
        cosine = cosine * square + (-1) ** n * (2 * math.pi) ** (2 * n) / math.factorial(2 * n)
        sine = sine * square + (-1) ** n * (2 * math.pi) ** (2 * n + 1) / math.factorial(2 * n + 1)
    return cosine, sine * turn


def rows_iota(shape):
    return lax.broadcasted_iota(jnp.int32, shape, len(shape) - 2)


def lanes_iota(shape):
    return lax.broadcasted_iota(jnp.int32, shape, len(shape) - 1)


def side_by_side(works):
    results = [None] * len(works)
    waiting = list(range(len(works)))
    while waiting:
        for n in list(waiting):
            try:
                next(works[n])
            except StopIteration as end:
                results[n] = end.value
                waiting.remove(n)
    return results


def pack_places(out_ref, places_ref, exports_ref, counts_ref, side):
    base = NH * BA
    out_ref[base : base + 8, :] = jnp.zeros((8, out_ref.shape[1]), f32)
    for s in range(NH):
        chosen = exports_ref[0, side, s]
        lane = side * base + s * BA
        found = places_ref[:, :BA]
        for b in range(1, NB):
            found = jnp.where(chosen == b, places_ref[:, b * BA : (b + 1) * BA], found)
        out_ref[base : base + 3, lane : lane + BA] = found
        live = jnp.where(s < counts_ref[0, side], 1.0, 0.0)
        out_ref[base + 3 : base + 4, lane : lane + BA] = jnp.full((1, BA), live, f32)


def pack_rows(out_ref, rows_ref, exports_ref, side):
    for s in range(NH):
        start = pl.multiple_of(exports_ref[0, side, s] * BA, BA)
        out_ref[s * BA : (s + 1) * BA, :] = rows_ref[pl.ds(start, BA), :]


def pack_kernel(features_ref, places_ref, exports_ref, counts_ref, up_ref, down_ref):
    for out_ref, side in ((up_ref, 0), (down_ref, 1)):
        pack_rows(out_ref, features_ref, exports_ref, side)
        pack_places(out_ref, places_ref, exports_ref, counts_ref, side)


def payload_kernel(
    features_ref, places_ref, charge_ref, anchor_ref, exports_ref, payload_ref, staged
):
    charge_rows = jnp.concatenate(
        [charge_ref[...], jnp.zeros((6, charge_ref.shape[1]), f32)], axis=0
    )
    charges = product(split(charge_rows), split(features_ref[...]), NT)
    chunks = features_ref.shape[0] // LANES
    for t in range(chunks):
        lane = slice(t * LANES, (t + 1) * LANES)
        for c in range(2):
            staged[c * chunks + t : c * chunks + t + 1, :] = charges[c : c + 1, lane]
        for d in range(3):
            row = (2 + d) * chunks + t
            staged[row : row + 1, :] = places_ref[d : d + 1, lane]
    anchors = anchor_ref[...].astype(f32)
    block = lanes_iota((3, LANES)) % (NB * BZ) // BZ
    spread = jnp.broadcast_to(anchors[:, :1], (3, LANES))
    for b in range(1, NB):
        spread = jnp.where(block == b, anchors[:, b : b + 1], spread)
    staged[5 * chunks : 5 * chunks + 3, :] = spread
    lane = lanes_iota((1, LANES))
    listed = jnp.zeros((1, LANES), jnp.int32)
    for side in range(2):
        for s in range(NH):
            listed = jnp.where(lane == side * NH + s, exports_ref[0, side, s], listed)
    staged[5 * chunks + 3 :, :] = listed.astype(f32)
    payload = staged[...]

    @pl.loop(0, payload_ref.shape[0])
    def _(domain):
        payload_ref[domain] = payload


def pair_terms(squared, live):
    softened = squared + soften
    near = jnp.exp(-2.0 * softened)
    if live is not None:
        near = near * live
    return near, jnp.exp(STEP * (softened * lax.rsqrt(softened)))


def squared_distance(columns, rows):
    total = None
    for d in range(3):
        delta = columns[:, d : d + 1] - rows[d : d + 1, :]
        total = delta * delta if total is None else total + delta * delta
    return total


def scaled_weights(weight_ref):
    return [weight_ref[k : k + 1, :] * float(FACTORS[k]) for k in range(NR)]


def place_columns(places_ref):
    atoms = places_ref.shape[1]
    return jnp.transpose(jnp.concatenate([places_ref[...], jnp.zeros((5, atoms), f32)], axis=0))


def ghost_messages(ghost_values_ref, places_ref, ghost_places, weight_ref):
    weights = scaled_weights(weight_ref)
    ghosts = 2 * NH * BA
    near, ratio = pair_terms(
        squared_distance(place_columns(places_ref), ghost_places[:, :ghosts]),
        ghost_places[3:4, :ghosts],
    )
    term = near

    def operands(k):
        nonlocal term
        after = term * ratio
        left = split(jnp.concatenate([term, after], axis=1))
        term = after * ratio
        values = ghost_values_ref[...]
        return left, split(
            jnp.concatenate([values * weights[k], values * weights[k + 1]], axis=0)
        )

    total = None
    ready = operands(0)
    for k in range(0, NR, 2):
        following = operands(k + 2) if k + 2 < NR else None
        part = product(*ready)
        total = part if total is None else total + part
        ready = following
    return total


def own_messages(values_ref, places_ref, weight_ref, out_ref):
    weights = scaled_weights(weight_ref)
    atoms = values_ref.shape[0]
    columns = place_columns(places_ref)
    half = lanes_iota((BA, 2 * BA)) >= BA
    partner = lanes_iota((BA, 2 * BA)) % BA
    other = (partner != rows_iota((BA, 2 * BA))).astype(f32)

    def one_block(b):
        rows = slice(b * BA, (b + 1) * BA)
        here = places_ref[:, rows]
        near, ratio = pair_terms(
            squared_distance(columns[rows], jnp.concatenate([here, here], axis=1)), other
        )
        term = jnp.where(half, near * ratio, near)
        ratio = ratio * ratio
        lefts, rights = [], []
        values = values_ref[rows, :]
        for k in range(0, NR, 2):
            lefts.append(term)
            rights.append(values * weights[k])
            rights.append(values * weights[k + 1])
            term = term * ratio
        left = split(jnp.concatenate(lefts, axis=1))
        right = split(jnp.concatenate(rights, axis=0))
        yield
        out_ref[rows, :] = product(left, right)

    blocks = atoms // BA
    for b in range(0, blocks, OWN_GROUP):
        side_by_side([one_block(b + n) for n in range(OWN_GROUP)])


def finish(hidden, messages, output_ref):
    scaled = messages * lax.rsqrt(
        jnp.mean(messages * messages, axis=-1, keepdims=True) + norm_epsilon
    )
    active = scaled / (1.0 + jnp.exp(-scaled))
    return hidden + product(split(active), split(output_ref[...]))


def first_own_kernel(
    features_ref, places_ref, value_one_ref, weight_ref, return_ref, value_two_ref,
    messages_ref, returned_ref,
    values,
):
    values[...] = product(split(features_ref[...]), split(value_one_ref[...]))
    own_messages(values, places_ref, weight_ref, messages_ref)
    return_rows = jnp.concatenate(
        [return_ref[...], jnp.zeros((6, return_ref.shape[1]), f32)], axis=0
    )
    returned_ref[...] = product(split(return_rows), split(value_two_ref[...]))


def fetched(sources, targets, arrived):
    copies = [
        pltpu.make_async_copy(source, target, arrived.at[n])
        for n, (source, target) in enumerate(zip(sources, targets))
    ]
    for copy in copies:
        copy.start()
    return copies


def first_layer_kernel(
    up_ref, down_ref, places_ref, value_one_ref, weight_ref, exports_ref,
    features_hbm, own_hbm, output_one_hbm, value_two_hbm,
    hidden_ref, values_two_ref, up_two_ref, down_two_ref, ghost_places_ref,
    ghost_values, features_ref, own_ref, output_one_ref, value_two_ref, arrived,
):
    copies = fetched(
        (features_hbm, own_hbm, output_one_hbm, value_two_hbm),
        (features_ref, own_ref, output_one_ref, value_two_ref),
        arrived,
    )
    base = NH * BA
    ghost_rows = jnp.concatenate([up_ref[:base, :], down_ref[:base, :]], axis=0)
    ghost_values[...] = product(split(ghost_rows), split(value_one_ref[...]))
    ghost_places_ref[...] = up_ref[base : base + 8, :] + down_ref[base : base + 8, :]
    messages = ghost_messages(ghost_values, places_ref, ghost_places_ref[...], weight_ref)
    for copy in copies:
        copy.wait()
    hidden_ref[...] = finish(features_ref[...], own_ref[...] + messages, output_one_ref)
    values_two_ref[...] = product(split(hidden_ref[...]), split(value_two_ref[...]))
    pack_rows(up_two_ref, values_two_ref, exports_ref, 0)
    pack_rows(down_two_ref, values_two_ref, exports_ref, 1)


def second_layer_kernel(
    values_ref, up_two_ref, down_two_ref, ghost_places_ref, places_ref, weight_ref,
    messages_ref,
    ghost_values,
):
    base = NH * BA
    ghost_values[:base, :] = up_two_ref[...]
    ghost_values[base:, :] = down_two_ref[...]
    own_messages(values_ref, places_ref, weight_ref, messages_ref)
    messages_ref[...] += ghost_messages(
        ghost_values, places_ref, ghost_places_ref[...], weight_ref
    )


def tail_kernel(
    received_ref, ghost_places_ref, places_ref, weight_ref, return_ref, returned_ref,
    messages_hbm, hidden_hbm, output_two_hbm,
    updated_ref,
    messages_ref, hidden_ref, output_two_ref, arrived,
):
    copies = fetched(
        (messages_hbm, hidden_hbm, output_two_hbm),
        (messages_ref, hidden_ref, output_two_ref),
        arrived,
    )
    atoms = hidden_ref.shape[0]
    ghosts = 2 * NH * BA
    potentials = jnp.sum(received_ref[...], axis=0)
    columns = jnp.transpose(potentials)
    ghost_places = ghost_places_ref[...]
    ghost_columns = jnp.transpose(ghost_places[:, :ghosts])
    own_columns = jnp.transpose(
        jnp.concatenate([places_ref[...], jnp.zeros((5, atoms), f32)], axis=0)
    )
    half = lanes_iota((BA, LANES)) >= BA
    other = (lanes_iota((BA, LANES)) % BA != rows_iota((BA, LANES))).astype(f32)
    ghost_potential = [
        jnp.concatenate([columns[c * BA : (c + 1) * BA, NB + s : NB + s + 1] for s in range(2 * NH)], axis=0)
        for c in range(2)
    ]
    pieces = []
    for t in range(atoms // LANES):
        lane = slice(t * LANES, (t + 1) * LANES)
        here = places_ref[:, lane]
        near, ratio = pair_terms(squared_distance(ghost_columns, here), ghost_columns[:, 3:4])
        squared = None
        own_potential = []
        for c in range(2):
            own_potential.append(
                jnp.where(
                    half,
                    columns[c * BA : (c + 1) * BA, 2 * t + 1 : 2 * t + 2],
                    columns[c * BA : (c + 1) * BA, 2 * t : 2 * t + 1],
                )
            )
        for d in range(3):
            first = own_columns[2 * t * BA : (2 * t + 1) * BA, d : d + 1]
            second = own_columns[(2 * t + 1) * BA : (2 * t + 2) * BA, d : d + 1]
            delta = jnp.where(half, second, first) - here[d : d + 1, :]
            squared = delta * delta if squared is None else squared + delta * delta
        own_near, own_ratio = pair_terms(squared, other)
        ratio = jnp.concatenate([ratio, own_ratio], axis=0)
        terms = [
            jnp.concatenate([near * ghost_potential[c], own_near * own_potential[c]], axis=0)
            for c in range(2)
        ]
        sums = [None] * (2 * NR)
        for start in range(0, ratio.shape[0], 8):
            tile = slice(start, start + 8)
            step = ratio[tile]
            for c in range(2):
                term = terms[c][tile]
                for k in range(NR):
                    at = 2 * k + c
                    sums[at] = term if sums[at] is None else sums[at] + term
                    if k + 1 < NR:
                        term = term * step
        pieces.append(
            jnp.concatenate([jnp.sum(total, axis=0, keepdims=True) for total in sums], axis=0)
        )
    gathered = jnp.transpose(jnp.concatenate(pieces, axis=1))
    spread = jnp.concatenate(
        [
            returned_ref[c : c + 1, :] * (weight_ref[k : k + 1, :] * float(FACTORS[k]))
            for k in range(NR)
            for c in range(2)
        ],
        axis=0,
    )
    for copy in copies:
        copy.wait()
    messages = messages_ref[...] + narrow_product(split(gathered), split(spread))
    back = [return_ref[c : c + 1, :] for c in range(2)]
    layer_input = jnp.concatenate(
        [
            hidden_ref[b * BA : (b + 1) * BA, :]
            + columns[:BA, b : b + 1] * back[0]
            + columns[BA:, b : b + 1] * back[1]
            for b in range(atoms // BA)
        ],
        axis=0,
    )
    updated_ref[...] = finish(layer_input, messages, output_two_ref)


def transform_tables(grid):
    half = grid // 2
    u = np.arange(grid)
    x = np.concatenate([np.arange(half + 1), np.arange(1, half)])
    angle = 2.0 * np.pi * (np.outer(u, x) % grid) / grid
    table = np.where(np.arange(grid)[None] <= half, np.cos(angle), np.sin(angle)).astype(np.float32)
    back = (table.T / float(grid) ** 3).astype(np.float32)

    def halves(value):
        high = value.astype(bf16)
        low = (value - high.astype(np.float32)).astype(bf16)
        return np.concatenate([high, high, low], axis=1)

    return halves(table), halves(back)


def reciprocal_kernel(
    grid, slabs, per_slab, second, depth,
    exports_ref, payload_ref, green_hbm, forward_ref, back_ref,
    out_ref,
    green_ref, green_arrived, planes_real, planes_imag, turns_high, turns_low, brick, carry,
    shift_cos, shift_sin, stage_cos, stage_sin, chosen, potential,
):
    green_copy = pltpu.make_async_copy(green_hbm, green_ref, green_arrived)
    green_copy.start()
    planes = (planes_real, planes_imag)
    domains = slabs * per_slab
    half = grid // 2
    pitch = grid + 8
    thick = grid // slabs
    starts = thick - BX + 1
    rows = 2 * second
    cells = per_slab * NB * BZ
    atoms = per_slab * NB * BA
    chunks = atoms // LANES
    own = NB * BA // LANES
    wide = depth
    first_v = (lax.axis_index("dom") * second).astype(f32)
    first_w = (lax.axis_index("rec") * green_hbm.shape[4]).astype(f32)
    period = float(grid)

    row = rows_iota((rows, 1))
    frequency = jnp.where(row >= second, row - second, row).astype(f32) + first_v
    cosine, sine = wave(jnp.broadcast_to(frequency, (rows, LANES)), period)
    shift_cos[...] = cosine
    shift_sin[...] = sine
    upper = rows_iota((rows, LANES)) >= second
    carry[...] = jnp.zeros(carry.shape, f32)
    left_half = lanes_iota((1, LANES)) < LANES // 2

    def atom_rows(slab, t):
        base = slab * per_slab + t // own
        return [payload_ref[base, q * own + t % own : q * own + t % own + 1, :] for q in range(5)]

    def windows(parts):
        cell = rows_iota((BY, LANES)).astype(f32)
        along_x = [jnp.exp(-((float(i) - parts[2] * 1.5) ** 2)) for i in range(BX)]
        along_y = jnp.exp(-((cell - parts[3] * 3.5) ** 2))
        along_z = jnp.exp(-((cell - parts[4] * 3.5) ** 2))
        return along_x, along_y, along_z

    def anchor(slab, dim):
        found = []
        for q in range(0, per_slab, 2):
            one = payload_ref[slab * per_slab + q, 5 * own + dim : 5 * own + dim + 1, :]
            two = payload_ref[slab * per_slab + q + 1, 5 * own + dim : 5 * own + dim + 1, :]
            found.append(jnp.where(left_half, one, two))
        return jnp.concatenate(found, axis=1) if len(found) > 1 else found[0]

    def spread_of(slab):
        both, pieces = [], []
        for t in range(chunks):
            parts = atom_rows(slab, t)
            along = windows(parts)
            pieces.append(jnp.where(left_half, along[2], 0.0))
            pieces.append(jnp.where(left_half, 0.0, along[2]))
            both.append((parts, along))
        return both, split(jnp.concatenate(pieces, axis=0))

    piece_of = lanes_iota((1, cells)) // (2 * BZ)

    def slab_masks(slab):
        start = anchor(slab, 0) - (slab * thick).astype(f32)
        return [(start == float(s)).astype(f32) for s in range(starts)]

    def deposit(slab, side):
        both, spread = spread_of(slab)
        lefts = []
        for parts, (along_x, along_y, _) in both:
            for c in range(2):
                for i in range(BX):
                    lefts.append((parts[c] * along_x[i]) * along_y)
        operand = split(jnp.concatenate(lefts, axis=0))
        yield
        found = product(operand, spread, NT)
        yield
        height = 2 * BX * BY
        total = found[:height]
        for t in range(1, chunks):
            total = jnp.where(piece_of == t, found[t * height : (t + 1) * height], total)
        brick[side] = total
        low_cell = anchor(slab, 2) + (lanes_iota((1, cells)) % BZ).astype(f32)
        ramp = rows_iota((8, cells)).astype(f32) + first_w
        cosine, sine = wave(ramp * low_cell, period)
        turn_cos, turn_sin = wave(8.0 * low_cell, period)
        for g in range(wide // 8):
            at = slice(g * 8, (g + 1) * 8)
            stage_cos[side, at, :] = cosine
            stage_sin[side, at, :] = sine
            cosine, sine = cosine * turn_cos - sine * turn_sin, cosine * turn_sin + sine * turn_cos
        cos_high, cos_low = split(stage_cos[side])
        sin_high, sin_low = split(stage_sin[side])
        for ref, c_part, s_part in ((turns_high, cos_high, sin_high), (turns_low, cos_low, sin_low)):
            ref[slab, :wide, :cells] = c_part
            ref[slab, :wide, cells:] = s_part
            ref[slab, wide:, :cells] = -s_part
            ref[slab, wide:, cells:] = c_part
        wide_cos = jnp.concatenate([shift_cos[...]] * (cells // LANES), axis=1)
        wide_sin = jnp.concatenate([shift_sin[...]] * (cells // LANES), axis=1)
        top = jnp.concatenate([upper] * (cells // LANES), axis=1) if cells > LANES else upper
        cosine, sine = wave(frequency * anchor(slab, 1), period)
        real = [jnp.zeros((rows, cells), f32)] * BX
        imag = [jnp.zeros((rows, cells), f32)] * BX
        for j in range(BY):
            for i in range(BX):
                low = brick[side, i * BY + j : i * BY + j + 1, :]
                high = brick[side, (BX + i) * BY + j : (BX + i) * BY + j + 1, :]
                weight = jnp.where(top, high, low)
                real[i] = real[i] + weight * cosine
                imag[i] = imag[i] - weight * sine
            if j + 1 < BY:
                cosine, sine = (
                    cosine * wide_cos - sine * wide_sin,
                    cosine * wide_sin + sine * wide_cos,
                )
        masks = slab_masks(slab)
        placed = []
        for x in range(thick):
            parts = []
            for source in (real, imag):
                total = None
                for i in range(BX):
                    if 0 <= x - i < starts:
                        piece = source[i] * masks[x - i]
                        total = piece if total is None else total + piece
                parts.append(total)
            placed.append(jnp.concatenate(parts, axis=1))
        operand = split(jnp.concatenate(placed, axis=0))
        yield
        return product(operand, (turns_high[slab], turns_low[slab]), NT)

    def put(x, value):
        for part, ref in enumerate(planes):
            ref[pl.ds(x, rows, stride=pitch), :] = value[:, part * wide : (part + 1) * wide]

    def get(x):
        return jnp.concatenate([ref[pl.ds(x, rows, stride=pitch), :] for ref in planes], axis=1)

    def swapped(value):
        return jnp.concatenate([value[:, wide:], -value[:, :wide]], axis=1)

    pairs = pairs_of(slabs, per_slab)

    @pl.loop(0, slabs // 2 // pairs)
    def _(step):
        first = [step * pairs + n for n in range(pairs)]
        both = [slab for m in first for slab in (m, slabs - 1 - m)]
        found = side_by_side([deposit(slab, side) for side, slab in enumerate(both)])
        last = carry[...]
        for n, m in enumerate(first):
            near, far = found[2 * n], found[2 * n + 1]
            for r in range(thick):
                x = m * thick + r
                one = near[r * rows : (r + 1) * rows]
                two = last if r == 0 else far[(thick - r) * rows : (thick - r + 1) * rows]
                put(x, one + two)
                put(half + x, swapped(one - two))
            last = far[:rows]
        carry[...] = last

    put(half, carry[...])
    green_copy.wait()

    def padded(kernel):
        gap = wide - kernel.shape[1]
        if gap == 0:
            return kernel
        return jnp.concatenate([kernel, jnp.zeros((kernel.shape[0], gap), f32)], axis=1)

    def transformed(table_ref, value):
        high, low = split(value)
        return lax.dot_general(
            table_ref[...], jnp.concatenate([high, low, high], axis=0), NN, preferred_element_type=f32
        )

    together = 2 if second % 2 == 0 else 1

    @pl.loop(0, second // together)
    def _(step):
        frequencies = [step * together + n for n in range(together)]
        places = [
            pl.ds(pl.multiple_of((c * second + v) * pitch, 8), grid)
            for v in frequencies
            for c in range(2)
        ]
        inside = jnp.concatenate([ref[place, :] for place in places for ref in planes], axis=1)
        spectrum = transformed(forward_ref, inside)
        outside = []
        for n, v in enumerate(frequencies):
            for c in range(2):
                zero, one = padded(green_ref[v, c, 0]), padded(green_ref[v, c, 1])
                for part in range(2):
                    at = (4 * n + part) * wide
                    outside.append(
                        zero * spectrum[:, at : at + wide]
                        + one * spectrum[:, at + 2 * wide : at + 3 * wide]
                    )
        result = transformed(back_ref, jnp.concatenate(outside, axis=1))
        for n, place in enumerate(places):
            for part, ref in enumerate(planes):
                at = (2 * n + part) * wide
                ref[place, :] = result[:, at : at + wide]

    def evaluate(slab, inputs, side):
        masks = slab_masks(slab)
        both, spread = spread_of(slab)
        operand = split(jnp.concatenate(inputs, axis=0))
        yield
        found = product(operand, (turns_high[slab], turns_low[slab]))
        yield
        twice = [jnp.concatenate([mask, mask], axis=1) for mask in masks]
        for i in range(BX):
            total = None
            for s in range(starts):
                piece = found[(s + i) * rows : (s + i + 1) * rows] * twice[s]
                total = piece if total is None else total + piece
            chosen[side, i * rows : (i + 1) * rows, :] = total
        cell = anchor(slab, 1) + rows_iota((BY, cells)).astype(f32)
        cosine, sine = wave(cell * first_v, period)
        turn_cos, turn_sin = wave(cell, period)
        sums = [jnp.zeros((BY, cells), f32)] * (2 * BX)
        for v in range(second):
            for c in range(2):
                for i in range(BX):
                    at = i * rows + c * second + v
                    sums[c * BX + i] = (
                        sums[c * BX + i]
                        + chosen[side, at : at + 1, :cells] * cosine
                        - chosen[side, at : at + 1, cells:] * sine
                    )
            if v + 1 < second:
                cosine, sine = cosine * turn_cos - sine * turn_sin, cosine * turn_sin + sine * turn_cos
        summed = jnp.concatenate(sums, axis=0)
        masked = [jnp.where(piece_of == t, summed, 0.0) for t in range(chunks)]
        operand = split(jnp.concatenate(masked, axis=0))
        yield
        at_atoms = product(operand, spread)
        yield
        for t in range(chunks):
            _, (along_x, along_y, _) = both[t]
            pair = []
            for c in range(2):
                total = None
                for i in range(BX):
                    at = (t * 2 * BX + c * BX + i) * BY
                    piece = at_atoms[at : at + BY] * along_x[i]
                    total = piece if total is None else total + piece
                pair.append(jnp.sum(total * along_y, axis=0, keepdims=True))
            one = jnp.where(left_half, pair[0], pltpu.roll(pair[1], LANES // 2, 1))
            two = jnp.where(left_half, pltpu.roll(pair[0], LANES // 2, 1), pair[1])
            potential[pl.ds(slab * per_slab * NB + 2 * t, 1), :] = one
            potential[pl.ds(slab * per_slab * NB + 2 * t + 1, 1), :] = two

    def straight(x):
        even = get(x)
        odd = get(jnp.minimum(half + x, grid - 1)) * jnp.where((x > 0) & (x < half), 1.0, 0.0)
        turned = jnp.concatenate([-odd[:, wide:], odd[:, :wide]], axis=1)
        return even + turned, even - turned

    @pl.loop(0, slabs // 2 // pairs)
    def _(step):
        works = []
        for n in range(pairs):
            m = step * pairs + n
            near, far = [], [None] * thick
            for r in range(thick):
                ahead, behind = straight(m * thick + r)
                near.append(ahead)
                if r > 0:
                    far[thick - r] = behind
            far[0] = straight(m * thick + thick)[1]
            works.append(evaluate(m, near, 2 * n))
            works.append(evaluate(slabs - 1 - m, far, 2 * n + 1))
        side_by_side(works)

    @pl.loop(0, domains)
    def _(domain):
        out_ref[domain, NB + 2 * NH :, :] = jnp.zeros((16 - NB - 2 * NH, LANES), f32)
        out_ref[domain, :NB, :] = potential[pl.ds(pl.multiple_of(domain * NB, NB), NB), :]
        below = lax.rem(domain + domains - 1, domains)
        above = lax.rem(domain + 1, domains)
        for s in range(NH):
            at = below * NB + exports_ref[below, s]
            out_ref[domain, NB + s : NB + s + 1, :] = potential[pl.ds(at, 1), :]
            at = above * NB + exports_ref[above, NH + s]
            out_ref[domain, NB + NH + s : NB + NH + s + 1, :] = potential[pl.ds(at, 1), :]


def pairs_of(slabs, per_slab):
    if per_slab <= 2 and slabs % 8 == 0:
        return 4
    return 2 if slabs % 4 == 0 else 1


def build_reciprocal(grid, slabs, per_slab, second, depth, depth_rows):
    domains = slabs * per_slab
    cells = per_slab * NB * BZ
    sides = 2 * pairs_of(slabs, per_slab)
    return pl.pallas_call(
        functools.partial(reciprocal_kernel, grid, slabs, per_slab, second, depth),
        in_specs=[SMEM, VMEM, ANY, VMEM, VMEM],
        out_specs=VMEM,
        out_shape=jax.ShapeDtypeStruct((domains, 16, LANES), f32),
        scratch_shapes=[
            pltpu.VMEM((second, 2, 2, grid, depth_rows), f32),
            pltpu.SemaphoreType.DMA,
            pltpu.VMEM((2 * second * (grid + 8), depth), f32),
            pltpu.VMEM((2 * second * (grid + 8), depth), f32),
            pltpu.VMEM((slabs, 2 * depth, 2 * cells), bf16),
            pltpu.VMEM((slabs, 2 * depth, 2 * cells), bf16),
            pltpu.VMEM((sides, 2 * BX * BY, cells), f32),
            pltpu.VMEM((2 * second, 2 * depth), f32),
            pltpu.VMEM((2 * second, LANES), f32),
            pltpu.VMEM((2 * second, LANES), f32),
            pltpu.VMEM((sides, depth, cells), f32),
            pltpu.VMEM((sides, depth, cells), f32),
            pltpu.VMEM((sides, BX * 2 * second, 2 * cells), f32),
            pltpu.VMEM((domains * NB, LANES), f32),
        ],
        compiler_params=params(),
    )


VMEM = pl.BlockSpec(memory_space=pltpu.VMEM)
SMEM = pl.BlockSpec(memory_space=pltpu.SMEM)
ANY = pl.BlockSpec(memory_space=pl.ANY)


def per_device(
    features,
    positions,
    value_one,
    output_one,
    radial_one,
    value_two,
    output_two,
    radial_two,
    charge_weight,
    return_weight,
    green_kernel,
    exports,
    export_counts,
    brick_anchor,
):
    axes = ("dom", "rec")
    slabs, per_slab = lax.axis_size("dom"), lax.axis_size("rec")
    domains = slabs * per_slab
    atoms, width = features.shape
    depth_rows, grid, second = green_kernel.shape[0], green_kernel.shape[3], green_kernel.shape[4]
    depth = -(-depth_rows // LANES) * LANES
    chunks = atoms // LANES
    payload_rows = 5 * chunks + 4
    base = NH * BA

    def shape(*dims):
        return jax.ShapeDtypeStruct(dims, f32)

    def around(rows, by):
        return lax.ppermute(rows, axes, [(i, (i + by) % domains) for i in range(domains)])

    up, down = pl.pallas_call(
        pack_kernel,
        in_specs=[VMEM] * 2 + [SMEM] * 2,
        out_specs=[VMEM] * 2,
        out_shape=[shape(base + 8, width), shape(base + 8, width)],
        compiler_params=params(),
    )(features, positions, exports, export_counts)

    up, down, features, green_kernel = lax.optimization_barrier((up, down, features, green_kernel))
    payload = pl.pallas_call(
        payload_kernel,
        in_specs=[VMEM] * 4 + [SMEM],
        out_specs=VMEM,
        out_shape=shape(domains, payload_rows, LANES),
        scratch_shapes=[pltpu.VMEM((payload_rows, LANES), f32)],
        compiler_params=params(),
    )(features, positions, charge_weight.T, brick_anchor, exports)
    up = around(up, 1)
    down = around(down, -1)
    own, returned = pl.pallas_call(
        first_own_kernel,
        in_specs=[VMEM] * 6,
        out_specs=[VMEM] * 2,
        out_shape=[shape(atoms, width), shape(8, width)],
        scratch_shapes=[pltpu.VMEM((atoms, width), f32)],
        compiler_params=params(),
    )(features, positions, value_one, radial_one, return_weight, value_two)
    green = jnp.transpose(green_kernel, (4, 1, 2, 3, 0))
    payload, own, green, up, down = lax.optimization_barrier((payload, own, green, up, down))
    everyone = lax.all_to_all(payload, axes, 0, 0, tiled=True)

    hidden, values_two, up_two, down_two, ghost_places = pl.pallas_call(
        first_layer_kernel,
        in_specs=[VMEM] * 5 + [SMEM] + [ANY] * 4,
        out_specs=[VMEM] * 5,
        out_shape=[
            shape(atoms, width), shape(atoms, width), shape(base, width), shape(base, width),
            shape(8, width),
        ],
        scratch_shapes=[
            pltpu.VMEM((2 * base, width), f32),
            pltpu.VMEM((atoms, width), f32),
            pltpu.VMEM((atoms, width), f32),
            pltpu.VMEM((width, width), f32),
            pltpu.VMEM((width, width), f32),
            pltpu.SemaphoreType.DMA((4,)),
        ],
        compiler_params=params(),
    )(up, down, positions, value_one, radial_one, exports, features, own, output_one, value_two)

    everyone, hidden = lax.optimization_barrier((everyone, hidden))
    up_two = around(up_two, 1)
    down_two = around(down_two, -1)

    all_exports = everyone[:, 5 * chunks + 3, :8].astype(jnp.int32)
    table, table_back = transform_tables(grid)
    outgoing = build_reciprocal(grid, slabs, per_slab, second, depth, depth_rows)(
        all_exports, everyone, green, table, table_back
    )

    outgoing, up_two, down_two = lax.optimization_barrier((outgoing, up_two, down_two))
    received = lax.all_to_all(outgoing, axes, 0, 0, tiled=True)

    messages = pl.pallas_call(
        second_layer_kernel,
        in_specs=[VMEM] * 6,
        out_specs=VMEM,
        out_shape=shape(atoms, width),
        scratch_shapes=[pltpu.VMEM((2 * base, width), f32)],
        compiler_params=params(),
    )(values_two, up_two, down_two, ghost_places, positions, radial_two)

    return pl.pallas_call(
        tail_kernel,
        in_specs=[VMEM] * 6 + [ANY] * 3,
        out_specs=VMEM,
        out_shape=shape(atoms, width),
        scratch_shapes=[
            pltpu.VMEM((atoms, width), f32),
            pltpu.VMEM((atoms, width), f32),
            pltpu.VMEM((width, width), f32),
            pltpu.SemaphoreType.DMA((3,)),
        ],
        compiler_params=params(),
    )(
        received, ghost_places, positions, radial_two, return_weight, returned,
        messages, hidden, output_two,
    )


def solution(mesh):
    placed = (
        P(("dom", "rec"), None),
        P(None, ("dom", "rec")),
        P(),
        P(),
        P(),
        P(),
        P(),
        P(),
        P(),
        P(),
        P("rec", None, None, None, "dom"),
        P(("dom", "rec"), None, None),
        P(("dom", "rec"), None),
        P(None, ("dom", "rec")),
    )
    return jax.shard_map(
        per_device, mesh=mesh, in_specs=placed, out_specs=P(("dom", "rec"), None), check_vma=False
    )
```
